1024 devices in a mesh: batch: 128 (over x, z), blk: 8 (over y, core).
Axes of the slice: x: 4, y: 4, z: 32, core: 2. Of those that a mesh axis runs over, the one named last changes fastest.
Arguments:
- basis_values: bfloat16 [128, 2048, 1024], P('batch'), may hold values from -6 to 6
- density: bfloat16 [4096, 128, 128], P(('batch', 'blk')), may hold values from -0.005859375 to 0.005859375
- tile_ids: int32 [128, 32], replicated, may hold values from 0 to 31, as said below
- extra_blocks: int32 [128, 4], P('batch'), may hold values from 0 to 3, as said below
- extra_count: int32 [128], P('batch'), may hold values from 0 to 4, as said below
- point_count: int32 [128], P('batch'), may hold values from 1024 to 2048, as said below
- core_density: float32 [128, 2048], P('batch'), may hold values from 0.5 to 2
- grid_weights: float32 [128, 2048], P('batch'), may hold values from 0.5 to 2
- point_pos: float32 [128, 2048], P('batch'), may hold values from 0 to 1, as said below
- external: float32 [128, 2048], P('batch'), may hold values from -1 to 1
Outputs:
- ham_tiles: float32 [4096, 128, 128], P(('batch', 'blk'))
- potential: float32 [128, 2048], P('batch')
The draws below stay inside these ranges and needn't reach their ends.
Inputs may be any that keep to these rules, and one draw needn't show every extreme that they name: `tile_ids`: row g names, for the 4 slots of each blk device in turn, the tile each holds; each of the 32 ids appears once in a row, and the first 2 slots of every device hold ids below 16. `extra_blocks`: the 4 entries of a row are different home blocks of group g + 1. `extra_count`: the last group lists none; every other group lists 2 or more; some group lists 4. The first point_count[g] points of group g are live; some group has all 2048. point_pos of group g lies in [g / 128, (g + 1) / 128).
All inputs are finite; a program needn't handle non-finite values.
Results may differ from the reference program's by a relative error of at most 0.0009.
The reference program's roundings to bfloat16 on the way (of `weighted`) count: a program that leaves them out, or rounds other values in their place, can miss the bound.
Values may be sent and summed in bfloat16 or wider, within the bound.
A program may use at most 32 MiB of HBM per device.

```python
import math
import jax
import jax.numpy as jnp
from jax import lax

NB = 128
HOME = 4
NXT = 4
NMOM = 4
GPTS = 2048
LB = 8
OWN_D = 2
OWN = 4
N_BATCH = 128
N_BLK = 8


def draw_tile_ids(key, part):
    key = jax.random.fold_in(key, 21)
    inner_keys = jax.random.split(jax.random.fold_in(key, 1), N_BATCH)
    cross_keys = jax.random.split(jax.random.fold_in(key, 2), N_BATCH)
    inner_perm = jax.vmap(lambda k: jax.random.permutation(k, HOME * HOME))(inner_keys)
    cross_perm = jax.vmap(lambda k: jax.random.permutation(k, HOME * HOME))(cross_keys) + HOME * HOME
    inner_part = inner_perm.reshape(N_BATCH, N_BLK, OWN_D)
    cross_part = cross_perm.reshape(N_BATCH, N_BLK, OWN_D)
    return jnp.concatenate([inner_part, cross_part], axis=2).reshape(N_BATCH, N_BLK * OWN).astype(jnp.int32)


def draw_extra_blocks(key, part):
    key = jax.random.fold_in(key, 22)
    group_keys = jax.random.split(key, N_BATCH)
    perms = jax.vmap(lambda k: jax.random.permutation(k, HOME))(group_keys)
    return perms[:, :NXT].astype(jnp.int32)


def draw_extra_count(key, part):
    key = jax.random.fold_in(key, 23)
    first_key, second_key = jax.random.split(key)
    counts = jax.random.randint(first_key, (N_BATCH,), 2, NXT + 1)
    chosen = jax.random.randint(second_key, (), 0, N_BATCH - 1)
    index_row = jnp.arange(N_BATCH)
    counts = jnp.where(index_row == chosen, NXT, counts)
    counts = jnp.where(index_row == N_BATCH - 1, 0, counts)
    return counts.astype(jnp.int32)


def draw_point_count(key, part):
    key = jax.random.fold_in(key, 24)
    first_key, second_key = jax.random.split(key)
    counts = jax.random.randint(first_key, (N_BATCH,), GPTS // 2, GPTS + 1)
    chosen = jax.random.randint(second_key, (), 0, N_BATCH)
    counts = jnp.where(jnp.arange(N_BATCH) == chosen, GPTS, counts)
    return counts.astype(jnp.int32)


def draw_point_pos(key, part):
    key = jax.random.fold_in(key, 25)
    offsets = jax.random.uniform(key, (N_BATCH, GPTS), jnp.float32, 0.0, 0.999)
    groups = jnp.arange(N_BATCH, dtype=jnp.float32)[:, None]
    return (groups + offsets) / N_BATCH


def block_levels(own_key, extent, cuts, smallest, top_value):
    factor_of, own = 1.0, jax.random.fold_in(own_key, 6)
    for dim, blocks in cuts:
        steps = jnp.exp(jax.random.uniform(jax.random.fold_in(own, dim), (blocks,), jnp.float32, smallest / len(cuts), top_value / len(cuts)))
        factor_of = factor_of * jnp.repeat(steps, extent[dim] // blocks).reshape([-1 if axis == dim else 1 for axis in range(len(extent))])
    return factor_of


def centred(key, dims, spread, reach, cuts=(), held_as=jnp.bfloat16):
    gain = block_levels(key, dims, cuts, -0.22, 0.18) if cuts else 1.0
    array = jax.random.normal(key, dims, jnp.float32) * spread * gain
    return jnp.minimum(jnp.maximum(array, -reach), reach).astype(held_as)


def setup_inputs(seed: int = 0) -> dict:
    streams_of = jax.random.split(jax.random.key(seed), 11)
    return {
        "basis_values": centred(streams_of[0], (N_BATCH, GPTS, LB * NB), 1.0, 6.0, ((0, 128),)),
        "density": centred(streams_of[1], (N_BATCH * N_BLK * OWN, NB, NB), (LB * LB * NB * NB) ** -0.5, 0.005859375, ((0, 1024),)),
        "tile_ids": draw_tile_ids(jax.random.fold_in(streams_of[10], 71), 0),
        "extra_blocks": draw_extra_blocks(jax.random.fold_in(streams_of[10], 71), 0),
        "extra_count": draw_extra_count(jax.random.fold_in(streams_of[10], 71), 0),
        "point_count": draw_point_count(jax.random.fold_in(streams_of[10], 71), 0),
        "core_density": jnp.clip(jnp.exp(math.log(2.0) - 1.3862944 * jax.random.uniform(streams_of[6], (N_BATCH, GPTS), jnp.float32) ** block_levels(streams_of[6], (N_BATCH, GPTS), ((0, 128),), -0.2, 0.2)), 0.5, 2.0),
        "grid_weights": jnp.clip(jnp.exp(math.log(2.0) - 1.3862944 * jax.random.uniform(streams_of[7], (N_BATCH, GPTS), jnp.float32) ** block_levels(streams_of[7], (N_BATCH, GPTS), ((0, 128),), -0.2, 0.2)), 0.5, 2.0),
        "point_pos": draw_point_pos(jax.random.fold_in(streams_of[10], 71), 0),
        "external": jnp.clip(jax.random.uniform(streams_of[9], (N_BATCH, GPTS), jnp.float32, -1.0, 1.0) * block_levels(streams_of[9], (N_BATCH, GPTS), ((0, 128),), -0.4, 0.0), -1.0, 1.0),
    }


EXCHANGE_COEF = 0.98
HARTREE_SCALE = 0.5


def next_position(block_id, extra_list, extra_num):
    live_slot = jnp.arange(NXT) < extra_num
    matches = (extra_list == block_id) & live_slot
    is_used = jnp.any(matches)
    position = HOME + jnp.sum(jnp.where(matches, jnp.arange(NXT), 0))
    return is_used, position.astype(jnp.int32)


def place_own(tile_id, extra_list, extra_num):
    inner_tile = tile_id < HOME * HOME
    local_id = jnp.where(inner_tile, tile_id, tile_id - HOME * HOME)
    row_block = local_id // HOME
    col_block = local_id % HOME
    col_used, col_pos = next_position(col_block, extra_list, extra_num)
    is_used = inner_tile | col_used
    factor = jnp.where(inner_tile, jnp.float32(1.0), jnp.float32(2.0))
    return is_used, row_block.astype(jnp.int32), jnp.where(inner_tile, col_block, col_pos).astype(jnp.int32), factor


def place_next(tile_id, extra_list, extra_num):
    row_used, row_pos = next_position(tile_id // HOME, extra_list, extra_num)
    col_used, col_pos = next_position(tile_id % HOME, extra_list, extra_num)
    is_used = row_used & col_used & (tile_id < HOME * HOME)
    return is_used, row_pos, col_pos, jnp.float32(1.0)


def rho_term(basis_vals, tile_data, placed):
    is_used, row_pos, col_pos, factor = placed
    left_cols = lax.dynamic_slice_in_dim(basis_vals, (row_pos * NB).astype(jnp.int32), NB, 1)
    right_cols = lax.dynamic_slice_in_dim(basis_vals, (col_pos * NB).astype(jnp.int32), NB, 1)
    product = jnp.dot(left_cols, tile_data, preferred_element_type=jnp.float32)
    return jnp.where(is_used, factor, jnp.float32(0.0)) * jnp.sum(product * right_cols.astype(jnp.float32), axis=1)


def ham_term(basis_vals, weighted, placed):
    is_used, row_pos, col_pos, factor = placed
    left_cols = lax.dynamic_slice_in_dim(basis_vals, (row_pos * NB).astype(jnp.int32), NB, 1)
    right_cols = lax.dynamic_slice_in_dim(weighted, (col_pos * NB).astype(jnp.int32), NB, 1)
    block_sum = lax.dot_general(left_cols, right_cols, (((0,), (0,)), ((), ())), preferred_element_type=jnp.float32)
    return jnp.where(is_used, jnp.float32(1.0), jnp.float32(0.0)) * block_sum


def reference(basis_values, density, tile_ids, extra_blocks, extra_count, point_count, core_density, grid_weights, point_pos, external):
    tiles_all = density.reshape(N_BATCH, N_BLK * OWN, NB, NB)

    def group_delta(group_idx):
        basis_vals = basis_values[group_idx]
        extra_list = extra_blocks[group_idx]
        extra_num = extra_count[group_idx]
        next_group = jnp.minimum(group_idx + 1, N_BATCH - 1)

        def own_one(tile_data, tile_id):
            return rho_term(basis_vals, tile_data, place_own(tile_id, extra_list, extra_num))

        def next_one(tile_data, tile_id):
            return rho_term(basis_vals, tile_data, place_next(tile_id, extra_list, extra_num))

        own_sum = jnp.sum(jax.vmap(own_one)(tiles_all[group_idx], tile_ids[group_idx]), axis=0)
        next_sum = jnp.sum(jax.vmap(next_one)(tiles_all[next_group], tile_ids[next_group]), axis=0)
        return own_sum + next_sum

    delta_rho = lax.map(group_delta, jnp.arange(N_BATCH, dtype=jnp.int32))
    rho_total = core_density + delta_rho
    live_mask = (jnp.arange(GPTS)[None, :] < point_count[:, None]).astype(jnp.float32)
    powers = jnp.stack([point_pos ** power for power in range(NMOM)])
    moments = jnp.sum(powers * (grid_weights * rho_total * live_mask)[None], axis=(1, 2)) / (N_BATCH * GPTS)
    far_field = jnp.sum(moments[:, None, None] * powers, axis=0)
    potential = external - EXCHANGE_COEF * rho_total * (1.0 + rho_total * rho_total) ** (-1.0 / 3.0) + HARTREE_SCALE * far_field
    quad_weight = grid_weights * potential * live_mask / GPTS

    def weigh(group_idx):
        return (quad_weight[group_idx][:, None] * basis_values[group_idx].astype(jnp.float32)).astype(jnp.bfloat16)

    def group_ham(group_idx):
        basis_vals = basis_values[group_idx]
        weighted = weigh(group_idx)
        prev_group = jnp.maximum(group_idx - 1, 0)
        prev_vals = basis_values[prev_group]
        prev_weighted = weigh(prev_group)
        ids_here = tile_ids[group_idx]

        def own_one(tile_id):
            return ham_term(basis_vals, weighted, place_own(tile_id, extra_blocks[group_idx], extra_count[group_idx]))

        def prev_one(tile_id):
            return ham_term(prev_vals, prev_weighted, place_next(tile_id, extra_blocks[prev_group], extra_count[prev_group]))

        own_ham = jax.vmap(own_one)(ids_here)
        prev_ham = jax.vmap(prev_one)(ids_here) * jnp.where(group_idx > 0, jnp.float32(1.0), jnp.float32(0.0))
        return own_ham + prev_ham

    ham_tiles = lax.map(group_ham, jnp.arange(N_BATCH, dtype=jnp.int32)).reshape(N_BATCH * N_BLK * OWN, NB, NB)
    return ham_tiles, potential
```

```python
import functools

import jax
import jax.numpy as jnp
from jax import lax
from jax.experimental import pallas as pl
from jax.experimental.pallas import tpu as pltpu
from jax.sharding import PartitionSpec as P

NB = 128
HOME = 4
NXT = 4
NMOM = 4
Z_LEN = 32
CHUNK = 256
LOADS = 4

EXCHANGE_COEF = 0.98
HARTREE_SCALE = 0.5
MESH = pl.DeviceIdType.MESH
F32 = jnp.float32
BF16 = jnp.bfloat16


def next_position(block_id, extra_list, extra_num):
    used = jnp.int32(0)
    position = jnp.int32(0)
    for slot in range(NXT):
        match = jnp.where((extra_list[slot] == block_id) & (slot < extra_num), 1, 0)
        used = used + match
        position = position + match * slot
    return used, position


def place_inner(tile_id, extra_list, extra_num):
    return jnp.int32(1), lax.div(tile_id, HOME), lax.rem(tile_id, HOME), jnp.int32(1)


def place_cross(tile_id, extra_list, extra_num):
    local_id = tile_id - HOME * HOME
    used, position = next_position(lax.rem(local_id, HOME), extra_list, extra_num)
    return used, lax.div(local_id, HOME), position, used * 2


def place_next(tile_id, extra_list, extra_num):
    row_used, row_pos = next_position(lax.div(tile_id, HOME), extra_list, extra_num)
    col_used, col_pos = next_position(lax.rem(tile_id, HOME), extra_list, extra_num)
    is_used = row_used * col_used
    return is_used, row_pos, col_pos, is_used


def pick(ref, span, first, number):
    blocks = [ref[span, (first + b) * NB : (first + b + 1) * NB] for b in range(HOME)]
    out = blocks[0]
    for b in range(1, HOME):
        out = jnp.where(number == b, blocks[b], out)
    return out


def kernel(
    sizes,
    ids_ref, extra_ref, count_ref, live_ref,
    basis_hbm, density_hbm, core_hbm, weight_hbm, pos_hbm, ext_hbm,
    ham_ref, pot_ref,
    basis, left, flipped, tiles, arrived, core_row, weight_row, pos_row, ext_row,
    acc, rho_own, rho_slots, mom_row, mom_slots, part_row, part_slots,
    weighted, quad, lent, returned,
    load_sem, small_sem, den_sem, rho_sem, mom_sem, part_sem, lent_sem,
):
    groups, members, z_len, points = sizes
    x_len = groups // z_len
    plane = x_len * members
    rows = points // NB
    owned = density_hbm.shape[0]
    inner_slots = owned // 2

    g = lax.axis_index("batch")
    m = lax.axis_index("blk")
    x = lax.div(g, z_len)
    z = lax.rem(g, z_len)
    here = x * members + m
    up = (lax.rem(g + 1, groups), m)
    down = (lax.rem(g + groups - 1, groups), m)

    def along_z(step):
        return (x * z_len + lax.rem(z + step, z_len), m)

    def in_plane(step):
        there = lax.rem(here + step, plane)
        return (lax.div(there, members) * z_len + z, lax.rem(there, members))

    def in_group(step):
        return (g, lax.rem(m + step, members))

    part = points // LOADS
    loads = []
    for i in range(LOADS):
        span = pl.ds(i * part, part)
        loads.append(pltpu.make_async_copy(basis_hbm.at[0, span], basis.at[span], load_sem.at[i]))
    small = [
        pltpu.make_async_copy(src, dst, small_sem.at[i])
        for i, (src, dst) in enumerate(
            [
                (density_hbm, tiles),
                (core_hbm, core_row),
                (weight_hbm, weight_row),
                (pos_hbm, pos_row),
                (ext_hbm, ext_row),
            ]
        )
    ]

    barrier = pltpu.get_barrier_semaphore()
    for neighbour in (up, down):
        pl.semaphore_signal(barrier, inc=1, device_id=neighbour, device_id_type=MESH)

    def greet_plane(step, carry):
        pl.semaphore_signal(barrier, inc=1, device_id=in_plane(step), device_id_type=MESH)
        return carry

    def greet_z(step, carry):
        pl.semaphore_signal(barrier, inc=1, device_id=along_z(step), device_id_type=MESH)
        return carry

    lax.fori_loop(1, z_len, greet_z, 0)
    lax.fori_loop(1, plane, greet_plane, 0)
    small[0].start()
    for copy in loads:
        copy.start()
    for copy in small[1:]:
        copy.start()

    extra_list = [extra_ref[0, slot] for slot in range(NXT)]
    extra_num = count_ref[0]
    g_up = lax.rem(g + 1, groups)
    own_places = [
        (place_inner if s < inner_slots else place_cross)(
            ids_ref[g, m * owned + s], extra_list, extra_num
        )
        for s in range(owned)
    ]
    next_places = [
        place_next(ids_ref[g_up, m * owned + s], extra_list, extra_num)
        for s in range(inner_slots)
    ]

    pl.semaphore_wait(barrier, (z_len - 1) + (plane - 1) + 2)

    density_copy = pltpu.make_async_remote_copy(
        src_ref=density_hbm.at[pl.ds(0, inner_slots)],
        dst_ref=arrived,
        send_sem=den_sem.at[0],
        recv_sem=den_sem.at[1],
        device_id=down,
        device_id_type=MESH,
    )
    density_copy.start()

    small[0].wait()
    for s in range(owned):
        factor = own_places[s][3].astype(F32)
        tiles[s] = (tiles[s].astype(F32) * factor).astype(BF16)

    places = own_places + next_places
    firsts = [(0, 0)] * inner_slots + [(0, HOME)] * (owned - inner_slots)
    firsts = firsts + [(HOME, HOME)] * inner_slots

    def tile_terms(span, stack, slots):
        total = None
        for i, s in enumerate(slots):
            _, row, col, _ = places[s]
            block = pick(basis, span, firsts[s][0], row)
            left[s, span, :] = block
            product = jnp.dot(block, stack[i], preferred_element_type=F32)
            term = product * pick(basis, span, firsts[s][1], col).astype(F32)
            total = term if total is None else total + term
        return total

    for i in range(LOADS):
        loads[i].wait()

    def own_chunk(c, carry):
        span = pl.ds(pl.multiple_of(c * CHUNK, CHUNK), CHUNK)
        acc[span, :] = tile_terms(span, tiles, range(owned))
        return carry

    lax.fori_loop(0, points // CHUNK, own_chunk, 0)
    for copy in small[1:]:
        copy.wait()

    density_copy.wait()
    for s in range(inner_slots):
        factor = next_places[s][3].astype(F32)
        arrived[s] = (arrived[s].astype(F32) * factor).astype(BF16)

    def next_chunk(c, carry):
        span = pl.ds(pl.multiple_of(c * CHUNK, CHUNK), CHUNK)
        total = acc[span, :] + tile_terms(span, arrived, range(owned, len(places)))
        for i in range(CHUNK // NB):
            turned = total[i * NB : (i + 1) * NB].T
            rho_own[pl.ds(c * (CHUNK // NB) + i, 1), :] = jnp.sum(turned, axis=0, keepdims=True)
        return carry

    lax.fori_loop(0, points // CHUNK, next_chunk, 0)

    rho_part = rho_own[...]
    pos = pos_row[...]
    index = lax.broadcasted_iota(jnp.int32, (rows, NB), 0) * NB + lax.broadcasted_iota(
        jnp.int32, (rows, NB), 1
    )
    live = jnp.where(index < live_ref[0], F32(1.0), F32(0.0))
    live_weight = weight_row[...] * live
    core_share = jnp.where(m == 0, F32(1.0), F32(0.0))
    term = live_weight * (rho_part + core_row[...] * core_share) * F32(1.0 / (groups * points))
    sums = []
    for power in range(NMOM):
        sums.append(jnp.sum(term, axis=0, keepdims=True))
        term = term * pos
    stack = jnp.concatenate(sums + [jnp.zeros((8 - NMOM, NB), F32)], axis=0)
    width = NB // NMOM
    stack = stack + pltpu.roll(stack, NB // 2, 1)
    stack = stack + pltpu.roll(stack, NB // 4, 1)
    quarter = lax.div(lax.broadcasted_iota(jnp.int32, (8, NB), 1), width)
    keep = quarter == lax.broadcasted_iota(jnp.int32, (8, NB), 0)
    row = jnp.sum(jnp.where(keep, stack, F32(0.0)), axis=0, keepdims=True)
    mom_row[...] = row
    mom_slots[z] = row

    def mom_copy(step):
        return pltpu.make_async_remote_copy(
            src_ref=mom_row,
            dst_ref=mom_slots.at[z],
            send_sem=mom_sem.at[0],
            recv_sem=mom_sem.at[1],
            device_id=along_z(step),
            device_id_type=MESH,
        )

    def send_mom(i, carry):
        step = z_len // 2 + lax.div(i + 1, 2) * (1 - 2 * lax.rem(i, 2))
        mom_copy(step).start()
        return carry

    lax.fori_loop(0, z_len - 1, send_mom, 0)

    rho_slots[m] = rho_part

    def rho_copy(step):
        return pltpu.make_async_remote_copy(
            src_ref=rho_own,
            dst_ref=rho_slots.at[m],
            send_sem=rho_sem.at[0],
            recv_sem=rho_sem.at[1],
            device_id=in_group(step),
            device_id_type=MESH,
        )

    def send_rho(step, carry):
        rho_copy(step).start()
        return carry

    lax.fori_loop(1, members, send_rho, 0)

    def flip_chunk(c, carry):
        span = pl.ds(pl.multiple_of(c * NB, NB), NB)
        for s, (_, _, col, _) in enumerate(places):
            flipped[s, :, span] = pick(basis, span, firsts[s][1], col).T
        return carry

    lax.fori_loop(0, rows, flip_chunk, 0)

    def wait_all(slots, count, sem, target):
        both = pltpu.make_async_remote_copy(
            src_ref=slots.at[pl.ds(0, count)],
            dst_ref=slots.at[pl.ds(0, count)],
            send_sem=sem.at[0],
            recv_sem=sem.at[1],
            device_id=target,
            device_id_type=MESH,
        )
        return both

    mom_all = wait_all(mom_slots, z_len - 1, mom_sem, along_z(1))
    mom_all.wait_recv()
    column = jnp.sum(mom_slots[...], axis=0)
    part_row[...] = column
    part_slots[here] = column

    def part_copy(step):
        return pltpu.make_async_remote_copy(
            src_ref=part_row,
            dst_ref=part_slots.at[here],
            send_sem=part_sem.at[0],
            recv_sem=part_sem.at[1],
            device_id=in_plane(step),
            device_id_type=MESH,
        )

    def send_part(step, carry):
        part_copy(step).start()
        return carry

    lax.fori_loop(1, plane, send_part, 0)

    rho_all = wait_all(rho_slots, members - 1, rho_sem, in_group(1))
    rho_all.wait_recv()
    rho = core_row[...] + jnp.sum(rho_slots[...], axis=0)
    local = ext_row[...] - F32(EXCHANGE_COEF) * rho * jnp.exp(
        F32(-1.0 / 3.0) * jnp.log(F32(1.0) + rho * rho)
    )
    scaled_weight = live_weight * F32(1.0 / points)

    part_all = wait_all(part_slots, plane - 1, part_sem, in_plane(1))
    part_all.wait_recv()
    total = jnp.sum(part_slots[...], axis=0)
    lane = lax.div(lax.broadcasted_iota(jnp.int32, (1, NB), 1), width)
    moments = [
        jnp.sum(jnp.where(lane == power, total, F32(0.0)), axis=1, keepdims=True)
        for power in range(NMOM)
    ]
    far = moments[3]
    for power in (2, 1, 0):
        far = far * pos + moments[power]
    potential = local + F32(HARTREE_SCALE) * far
    pot_ref[...] = potential
    quad[...] = scaled_weight * potential

    def ham_tile(s):
        for i in range(rows):
            span = slice(i * NB, (i + 1) * NB)
            block = flipped[s, :, span].astype(F32)
            weighted[:, span] = (block * quad[i : i + 1, :]).astype(BF16)
        turned = jnp.dot(weighted[...], left[s], preferred_element_type=F32)
        return turned.T * places[s][0].astype(F32)

    lent_copies = []
    for s in range(inner_slots):
        lent[s] = ham_tile(owned + s)
        copy = pltpu.make_async_remote_copy(
            src_ref=lent.at[s],
            dst_ref=returned.at[s],
            send_sem=lent_sem.at[0, s],
            recv_sem=lent_sem.at[1, s],
            device_id=up,
            device_id_type=MESH,
        )
        copy.start()
        lent_copies.append(copy)
    for s in range(owned):
        ham_ref[s] = ham_tile(s)
    for s in range(inner_slots):
        lent_copies[s].wait()
        ham_ref[s] = ham_ref[s] + returned[s]

    mom_all.wait_send()
    rho_all.wait_send()
    part_all.wait_send()


def body(
    basis_values, density, tile_ids, extra_blocks, extra_count, point_count,
    core_density, grid_weights, point_pos, external,
):
    groups = lax.axis_size("batch")
    members = lax.axis_size("blk")
    points = basis_values.shape[1]
    owned = density.shape[0]
    inner_slots = owned // 2
    rows = points // NB
    columns = basis_values.shape[2]
    z_len = min(Z_LEN, groups)
    plane = groups // z_len * members
    smem = pl.BlockSpec(memory_space=pltpu.SMEM)
    anywhere = pl.BlockSpec(memory_space=pl.ANY)
    vmem = pl.BlockSpec(memory_space=pltpu.VMEM)
    ham_tiles, potential = pl.pallas_call(
        functools.partial(kernel, (groups, members, z_len, points)),
        out_shape=(
            jax.ShapeDtypeStruct((owned, NB, NB), F32),
            jax.ShapeDtypeStruct((rows, NB), F32),
        ),
        in_specs=[smem] * 4 + [anywhere] * 6,
        out_specs=(vmem, vmem),
        scratch_shapes=[
            pltpu.VMEM((points, columns), BF16),
            pltpu.VMEM((owned + inner_slots, points, NB), BF16),
            pltpu.VMEM((owned + inner_slots, NB, points), BF16),
            pltpu.VMEM((owned, NB, NB), BF16),
            pltpu.VMEM((inner_slots, NB, NB), BF16),
            pltpu.VMEM((rows, NB), F32),
            pltpu.VMEM((rows, NB), F32),
            pltpu.VMEM((rows, NB), F32),
            pltpu.VMEM((rows, NB), F32),
            pltpu.VMEM((points, NB), F32),
            pltpu.VMEM((rows, NB), F32),
            pltpu.VMEM((members, rows, NB), F32),
            pltpu.VMEM((1, NB), F32),
            pltpu.VMEM((z_len, 1, NB), F32),
            pltpu.VMEM((1, NB), F32),
            pltpu.VMEM((plane, 1, NB), F32),
            pltpu.VMEM((NB, points), BF16),
            pltpu.VMEM((rows, NB), F32),
            pltpu.VMEM((inner_slots, NB, NB), F32),
            pltpu.VMEM((inner_slots, NB, NB), F32),
            pltpu.SemaphoreType.DMA((LOADS,)),
            pltpu.SemaphoreType.DMA((5,)),
            pltpu.SemaphoreType.DMA((2,)),
            pltpu.SemaphoreType.DMA((2,)),
            pltpu.SemaphoreType.DMA((2,)),
            pltpu.SemaphoreType.DMA((2,)),
            pltpu.SemaphoreType.DMA((2, inner_slots)),
        ],
        compiler_params=pltpu.CompilerParams(
            collective_id=0, has_side_effects=True, vmem_limit_bytes=40 * 1024 * 1024
        ),
        name="density_hamiltonian",
    )(
        tile_ids, extra_blocks, extra_count, point_count,
        basis_values, density,
        core_density.reshape(rows, NB), grid_weights.reshape(rows, NB),
        point_pos.reshape(rows, NB), external.reshape(rows, NB),
    )
    return ham_tiles, potential.reshape(1, points)


def solution(mesh):
    return jax.shard_map(
        body,
        mesh=mesh,
        in_specs=(
            P("batch", None, None),
            P(("batch", "blk"), None, None),
            P(),
            P("batch", None),
            P("batch"),
            P("batch"),
            P("batch", None),
            P("batch", None),
            P("batch", None),
            P("batch", None),
        ),
        out_specs=(P(("batch", "blk"), None, None), P("batch", None)),
        check_vma=False,
    )
```

```python
import functools

import jax
import jax.numpy as jnp
from jax import lax
from jax.experimental import pallas as pl
from jax.experimental.pallas import tpu as pltpu
from jax.sharding import PartitionSpec as P

NB = 128
HOME = 4
NXT = 4
NMOM = 4
Z_LEN = 32
CHUNK = 256
LOADS = 4
VMEM_BYTES = 60 * 1024 * 1024

EXCHANGE_COEF = 0.98
HARTREE_SCALE = 0.5
MESH = pl.DeviceIdType.MESH
F32 = jnp.float32
BF16 = jnp.bfloat16


def next_position(block_id, extra_list, extra_num):
    used = jnp.int32(0)
    position = jnp.int32(0)
    for slot in range(NXT):
        match = jnp.where((extra_list[slot] == block_id) & (slot < extra_num), 1, 0)
        used = used + match
        position = position + match * slot
    return used, position


def place_inner(tile_id, extra_list, extra_num):
    return jnp.int32(1), lax.div(tile_id, HOME), lax.rem(tile_id, HOME), jnp.int32(1)


def place_cross(tile_id, extra_list, extra_num):
    local_id = tile_id - HOME * HOME
    used, position = next_position(lax.rem(local_id, HOME), extra_list, extra_num)
    return used, lax.div(local_id, HOME), position, used * 2


def place_next(tile_id, extra_list, extra_num):
    row_used, row_pos = next_position(lax.div(tile_id, HOME), extra_list, extra_num)
    col_used, col_pos = next_position(lax.rem(tile_id, HOME), extra_list, extra_num)
    is_used = row_used * col_used
    return is_used, row_pos, col_pos, is_used


def pick(ref, span, first, number):
    blocks = [ref[span, (first + b) * NB : (first + b + 1) * NB] for b in range(HOME)]
    out = blocks[0]
    for b in range(1, HOME):
        out = jnp.where(number == b, blocks[b], out)
    return out


def kernel(
    sizes,
    ids_hbm, extra_hbm, count_hbm, live_hbm,
    basis_hbm, density_hbm, core_hbm, weight_hbm, pos_hbm, ext_hbm,
    ham_hbm, pot_hbm,
    ids_ref, extra_ref, count_ref, live_ref,
    basis, left, flipped, tiles, arrived, core_row, weight_row, pos_row, ext_row,
    acc, rho_own, rho_slots, mom_row, mom_slots, part_row, part_slots,
    weighted, quad, lent, returned, ham_ref, pot_ref,
    load_sem, small_sem, index_sem, den_sem, rho_sem, mom_sem, part_sem, lent_sem, out_sem,
):
    groups, members, z_len, points = sizes
    x_len = groups // z_len
    plane = x_len * members
    rows = points // NB
    owned = density_hbm.shape[0]
    inner_slots = owned // 2

    g = lax.axis_index("batch")
    m = lax.axis_index("blk")
    x = lax.div(g, z_len)
    z = lax.rem(g, z_len)
    here = x * members + m
    up = (lax.rem(g + 1, groups), m)
    down = (lax.rem(g + groups - 1, groups), m)

    def along_z(step):
        return (x * z_len + lax.rem(z + step, z_len), m)

    def in_plane(step):
        there = lax.rem(here + step, plane)
        return (lax.div(there, members) * z_len + z, lax.rem(there, members))

    def in_group(step):
        return (g, lax.rem(m + step, members))

    part = points // LOADS
    loads = []
    for i in range(LOADS):
        span = pl.ds(i * part, part)
        loads.append(pltpu.make_async_copy(basis_hbm.at[0, span], basis.at[span], load_sem.at[i]))
    small = [
        pltpu.make_async_copy(src, dst, small_sem.at[i])
        for i, (src, dst) in enumerate(
            [
                (density_hbm, tiles),
                (core_hbm, core_row),
                (weight_hbm, weight_row),
                (pos_hbm, pos_row),
                (ext_hbm, ext_row),
            ]
        )
    ]

    g_up = lax.rem(g + 1, groups)
    tiny = [
        pltpu.make_async_copy(src, dst, index_sem.at[i])
        for i, (src, dst) in enumerate(
            [
                (ids_hbm, ids_ref),
                (extra_hbm, extra_ref),
                (count_hbm, count_ref),
                (live_hbm, live_ref),
            ]
        )
    ]

    barrier = pltpu.get_barrier_semaphore()
    for neighbour in (up, down):
        pl.semaphore_signal(barrier, inc=1, device_id=neighbour, device_id_type=MESH)

    def greet_plane(step, carry):
        pl.semaphore_signal(barrier, inc=1, device_id=in_plane(step), device_id_type=MESH)
        return carry

    def greet_z(step, carry):
        pl.semaphore_signal(barrier, inc=1, device_id=along_z(step), device_id_type=MESH)
        return carry

    lax.fori_loop(1, z_len, greet_z, 0)
    lax.fori_loop(1, plane, greet_plane, 0)
    for copy in tiny:
        copy.start()
    small[0].start()
    for copy in loads:
        copy.start()
    for copy in small[1:]:
        copy.start()

    for copy in tiny:
        copy.wait()
    extra_list = [extra_ref[0, slot] for slot in range(NXT)]
    extra_num = count_ref[0, 0]
    own_places = [
        (place_inner if s < inner_slots else place_cross)(
            ids_ref[m * owned + s, g], extra_list, extra_num
        )
        for s in range(owned)
    ]
    next_places = [
        place_next(ids_ref[m * owned + s, g_up], extra_list, extra_num)
        for s in range(inner_slots)
    ]

    pl.semaphore_wait(barrier, (z_len - 1) + (plane - 1) + 2)

    density_copy = pltpu.make_async_remote_copy(
        src_ref=density_hbm.at[pl.ds(0, inner_slots)],
        dst_ref=arrived,
        send_sem=den_sem.at[0],
        recv_sem=den_sem.at[1],
        device_id=down,
        device_id_type=MESH,
    )
    density_copy.start()

    small[0].wait()
    for s in range(owned):
        factor = own_places[s][3].astype(F32)
        tiles[s] = (tiles[s].astype(F32) * factor).astype(BF16)

    places = own_places + next_places
    firsts = [(0, 0)] * inner_slots + [(0, HOME)] * (owned - inner_slots)
    firsts = firsts + [(HOME, HOME)] * inner_slots

    def tile_terms(span, stack, slots):
        total = None
        for i, s in enumerate(slots):
            _, row, col, _ = places[s]
            block = pick(basis, span, firsts[s][0], row)
            left[s, span, :] = block
            product = jnp.dot(block, stack[i], preferred_element_type=F32)
            term = product * pick(basis, span, firsts[s][1], col).astype(F32)
            total = term if total is None else total + term
        return total

    for i in range(LOADS):
        loads[i].wait()
        span = slice(i * part, (i + 1) * part)
        acc[span, :] = tile_terms(span, tiles, range(owned))
    for copy in small[1:]:
        copy.wait()

    density_copy.wait()
    for s in range(inner_slots):
        factor = next_places[s][3].astype(F32)
        arrived[s] = (arrived[s].astype(F32) * factor).astype(BF16)

    for c in range(points // CHUNK):
        span = slice(c * CHUNK, (c + 1) * CHUNK)
        total = acc[span, :] + tile_terms(span, arrived, range(owned, len(places)))
        for i in range(CHUNK // NB):
            turned = total[i * NB : (i + 1) * NB].T
            at = c * (CHUNK // NB) + i
            rho_own[at : at + 1, :] = jnp.sum(turned, axis=0, keepdims=True)

    rho_part = rho_own[...]
    pos = pos_row[...]
    index = lax.broadcasted_iota(jnp.int32, (rows, NB), 0) * NB + lax.broadcasted_iota(
        jnp.int32, (rows, NB), 1
    )
    live = jnp.where(index < live_ref[0, 0], F32(1.0), F32(0.0))
    live_weight = weight_row[...] * live
    core_share = jnp.where(m == 0, F32(1.0), F32(0.0))
    term = live_weight * (rho_part + core_row[...] * core_share) * F32(1.0 / (groups * points))
    sums = []
    for power in range(NMOM):
        sums.append(jnp.sum(term, axis=0, keepdims=True))
        term = term * pos
    stack = jnp.concatenate(sums + [jnp.zeros((8 - NMOM, NB), F32)], axis=0)
    width = NB // NMOM
    stack = stack + pltpu.roll(stack, NB // 2, 1)
    stack = stack + pltpu.roll(stack, NB // 4, 1)
    quarter = lax.div(lax.broadcasted_iota(jnp.int32, (8, NB), 1), width)
    keep = quarter == lax.broadcasted_iota(jnp.int32, (8, NB), 0)
    row = jnp.sum(jnp.where(keep, stack, F32(0.0)), axis=0, keepdims=True)
    mom_row[...] = row
    mom_slots[z] = row

    def mom_copy(step):
        return pltpu.make_async_remote_copy(
            src_ref=mom_row,
            dst_ref=mom_slots.at[z],
            send_sem=mom_sem.at[0],
            recv_sem=mom_sem.at[1],
            device_id=along_z(step),
            device_id_type=MESH,
        )

    def send_mom(i, carry):
        step = z_len // 2 + lax.div(i + 1, 2) * (1 - 2 * lax.rem(i, 2))
        mom_copy(step).start()
        return carry

    lax.fori_loop(0, z_len - 1, send_mom, 0)

    rho_slots[m] = rho_part

    def rho_copy(step):
        return pltpu.make_async_remote_copy(
            src_ref=rho_own,
            dst_ref=rho_slots.at[m],
            send_sem=rho_sem.at[0],
            recv_sem=rho_sem.at[1],
            device_id=in_group(step),
            device_id_type=MESH,
        )

    def send_rho(step, carry):
        rho_copy(step).start()
        return carry

    lax.fori_loop(1, members, send_rho, 0)

    def flip_chunk(c, carry):
        span = pl.ds(pl.multiple_of(c * NB, NB), NB)
        for s, (_, _, col, _) in enumerate(places):
            flipped[s, :, span] = pick(basis, span, firsts[s][1], col).T
        return carry

    lax.fori_loop(0, rows, flip_chunk, 0)

    def wait_all(slots, count, sem, target):
        both = pltpu.make_async_remote_copy(
            src_ref=slots.at[pl.ds(0, count)],
            dst_ref=slots.at[pl.ds(0, count)],
            send_sem=sem.at[0],
            recv_sem=sem.at[1],
            device_id=target,
            device_id_type=MESH,
        )
        return both

    mom_all = wait_all(mom_slots, z_len - 1, mom_sem, along_z(1))
    mom_all.wait_recv()
    column = jnp.sum(mom_slots[...], axis=0)
    part_row[...] = column
    part_slots[here] = column

    def part_copy(step):
        return pltpu.make_async_remote_copy(
            src_ref=part_row,
            dst_ref=part_slots.at[here],
            send_sem=part_sem.at[0],
            recv_sem=part_sem.at[1],
            device_id=in_plane(step),
            device_id_type=MESH,
        )

    def send_part(step, carry):
        part_copy(step).start()
        return carry

    lax.fori_loop(1, plane, send_part, 0)

    rho_all = wait_all(rho_slots, members - 1, rho_sem, in_group(1))
    rho_all.wait_recv()
    rho = core_row[...] + jnp.sum(rho_slots[...], axis=0)
    local = ext_row[...] - F32(EXCHANGE_COEF) * rho * jnp.exp(
        F32(-1.0 / 3.0) * jnp.log(F32(1.0) + rho * rho)
    )
    scaled_weight = live_weight * F32(1.0 / points)

    part_all = wait_all(part_slots, plane - 1, part_sem, in_plane(1))
    part_all.wait_recv()
    total = jnp.sum(part_slots[...], axis=0)
    lane = lax.div(lax.broadcasted_iota(jnp.int32, (1, NB), 1), width)
    moments = [
        jnp.sum(jnp.where(lane == power, total, F32(0.0)), axis=1, keepdims=True)
        for power in range(NMOM)
    ]
    far = moments[3]
    for power in (2, 1, 0):
        far = far * pos + moments[power]
    potential = local + F32(HARTREE_SCALE) * far
    pot_ref[...] = potential
    pot_out = pltpu.make_async_copy(pot_ref, pot_hbm, out_sem.at[owned])
    pot_out.start()
    quad[...] = scaled_weight * potential

    def ham_tile(s):
        for i in range(rows):
            span = slice(i * NB, (i + 1) * NB)
            block = flipped[s, :, span].astype(F32)
            weighted[:, span] = (block * quad[i : i + 1, :]).astype(BF16)
        turned = jnp.dot(weighted[...], left[s], preferred_element_type=F32)
        return turned.T * places[s][0].astype(F32)

    lent_copies = []
    for s in range(inner_slots):
        lent[s] = ham_tile(owned + s)
        copy = pltpu.make_async_remote_copy(
            src_ref=lent.at[s],
            dst_ref=returned.at[s],
            send_sem=lent_sem.at[0, s],
            recv_sem=lent_sem.at[1, s],
            device_id=up,
            device_id_type=MESH,
        )
        copy.start()
        lent_copies.append(copy)
    ham_out = [
        pltpu.make_async_copy(ham_ref.at[s], ham_hbm.at[s], out_sem.at[s]) for s in range(owned)
    ]
    for s in range(owned):
        ham_ref[s] = ham_tile(s)
        if s >= inner_slots:
            ham_out[s].start()
    for s in range(inner_slots):
        lent_copies[s].wait()
        ham_ref[s] = ham_ref[s] + returned[s]
        ham_out[s].start()
    for copy in ham_out + [pot_out]:
        copy.wait()

    mom_all.wait_send()
    rho_all.wait_send()
    part_all.wait_send()


def body(
    basis_values, density, tile_ids, extra_blocks, extra_count, point_count,
    core_density, grid_weights, point_pos, external,
):
    groups = lax.axis_size("batch")
    members = lax.axis_size("blk")
    points = basis_values.shape[1]
    owned = density.shape[0]
    inner_slots = owned // 2
    rows = points // NB
    columns = basis_values.shape[2]
    z_len = min(Z_LEN, groups)
    plane = groups // z_len * members
    hbm = pl.BlockSpec(memory_space=pltpu.HBM)
    ham_tiles, potential = pl.pallas_call(
        functools.partial(kernel, (groups, members, z_len, points)),
        out_shape=(
            jax.ShapeDtypeStruct((owned, NB, NB), F32),
            jax.ShapeDtypeStruct((rows, NB), F32),
        ),
        in_specs=[hbm] * 10,
        out_specs=(hbm, hbm),
        scratch_shapes=[
            pltpu.SMEM((members * owned, groups), jnp.int32),
            pltpu.SMEM((1, NXT), jnp.int32),
            pltpu.SMEM((1, 1), jnp.int32),
            pltpu.SMEM((1, 1), jnp.int32),
            pltpu.VMEM((points, columns), BF16),
            pltpu.VMEM((owned + inner_slots, points, NB), BF16),
            pltpu.VMEM((owned + inner_slots, NB, points), BF16),
            pltpu.VMEM((owned, NB, NB), BF16),
            pltpu.VMEM((inner_slots, NB, NB), BF16),
            pltpu.VMEM((rows, NB), F32),
            pltpu.VMEM((rows, NB), F32),
            pltpu.VMEM((rows, NB), F32),
            pltpu.VMEM((rows, NB), F32),
            pltpu.VMEM((points, NB), F32),
            pltpu.VMEM((rows, NB), F32),
            pltpu.VMEM((members, rows, NB), F32),
            pltpu.VMEM((1, NB), F32),
            pltpu.VMEM((z_len, 1, NB), F32),
            pltpu.VMEM((1, NB), F32),
            pltpu.VMEM((plane, 1, NB), F32),
            pltpu.VMEM((NB, points), BF16),
            pltpu.VMEM((rows, NB), F32),
            pltpu.VMEM((inner_slots, NB, NB), F32),
            pltpu.VMEM((inner_slots, NB, NB), F32),
            pltpu.VMEM((owned, NB, NB), F32),
            pltpu.VMEM((rows, NB), F32),
            pltpu.SemaphoreType.DMA((LOADS,)),
            pltpu.SemaphoreType.DMA((5,)),
            pltpu.SemaphoreType.DMA((4,)),
            pltpu.SemaphoreType.DMA((2,)),
            pltpu.SemaphoreType.DMA((2,)),
            pltpu.SemaphoreType.DMA((2,)),
            pltpu.SemaphoreType.DMA((2,)),
            pltpu.SemaphoreType.DMA((2, inner_slots)),
            pltpu.SemaphoreType.DMA((owned + 1,)),
        ],
        compiler_params=pltpu.CompilerParams(
            collective_id=0, has_side_effects=True, vmem_limit_bytes=VMEM_BYTES
        ),
        name="density_hamiltonian",
    )(
        tile_ids.T, extra_blocks, extra_count.reshape(1, 1), point_count.reshape(1, 1),
        basis_values, density,
        core_density.reshape(rows, NB), grid_weights.reshape(rows, NB),
        point_pos.reshape(rows, NB), external.reshape(rows, NB),
    )
    return ham_tiles, potential.reshape(1, points)


def solution(mesh):
    return jax.shard_map(
        body,
        mesh=mesh,
        in_specs=(
            P("batch", None, None),
            P(("batch", "blk"), None, None),
            P(),
            P("batch", None),
            P("batch"),
            P("batch"),
            P("batch", None),
            P("batch", None),
            P("batch", None),
            P("batch", None),
        ),
        out_specs=(P(("batch", "blk"), None, None), P("batch", None)),
        check_vma=False,
    )
```

```python
import functools

import jax
import jax.numpy as jnp
from jax import lax
from jax.experimental import pallas as pl
from jax.experimental.pallas import tpu as pltpu
from jax.sharding import PartitionSpec as P

NB = 128
HOME = 4
NXT = 4
NMOM = 4
Z_LEN = 32
CHUNK = 256
LOADS = 4
VMEM_BYTES = 60 * 1024 * 1024

EXCHANGE_COEF = 0.98
HARTREE_SCALE = 0.5
MESH = pl.DeviceIdType.MESH
F32 = jnp.float32
BF16 = jnp.bfloat16


def next_position(block_id, extra_list, extra_num):
    used = jnp.int32(0)
    position = jnp.int32(0)
    for slot in range(NXT):
        match = jnp.where((extra_list[slot] == block_id) & (slot < extra_num), 1, 0)
        used = used + match
        position = position + match * slot
    return used, position


def place_inner(tile_id, extra_list, extra_num):
    return jnp.int32(1), lax.div(tile_id, HOME), lax.rem(tile_id, HOME), jnp.int32(1)


def place_cross(tile_id, extra_list, extra_num):
    local_id = tile_id - HOME * HOME
    used, position = next_position(lax.rem(local_id, HOME), extra_list, extra_num)
    return used, lax.div(local_id, HOME), position, used * 2


def place_next(tile_id, extra_list, extra_num):
    row_used, row_pos = next_position(lax.div(tile_id, HOME), extra_list, extra_num)
    col_used, col_pos = next_position(lax.rem(tile_id, HOME), extra_list, extra_num)
    is_used = row_used * col_used
    return is_used, row_pos, col_pos, is_used


def pick(ref, span, first, number):
    blocks = [ref[span, (first + b) * NB : (first + b + 1) * NB] for b in range(HOME)]
    out = blocks[0]
    for b in range(1, HOME):
        out = jnp.where(number == b, blocks[b], out)
    return out


def kernel(
    sizes,
    ids_hbm, extra_hbm, count_hbm, live_hbm,
    basis_hbm, density_hbm, core_hbm, weight_hbm, pos_hbm, ext_hbm,
    ham_hbm, returned, pot_hbm,
    ids_ref, extra_ref, count_ref, live_ref,
    basis, left, flipped, tiles, arrived, core_row, weight_row, pos_row, ext_row,
    acc, rho_own, rho_slots, mom_row, mom_slots, part_row, part_slots,
    weighted, quad, lent, ham_ref, pot_ref,
    load_sem, small_sem, index_sem, den_sem, rho_sem, mom_sem, part_sem, lent_sem, out_sem,
):
    groups, members, z_len, points = sizes
    x_len = groups // z_len
    plane = x_len * members
    rows = points // NB
    owned = density_hbm.shape[0]
    inner_slots = owned // 2

    g = lax.axis_index("batch")
    m = lax.axis_index("blk")
    x = lax.div(g, z_len)
    z = lax.rem(g, z_len)
    here = x * members + m
    up = (lax.rem(g + 1, groups), m)
    down = (lax.rem(g + groups - 1, groups), m)

    def along_z(step):
        return (x * z_len + lax.rem(z + step, z_len), m)

    def in_plane(step):
        there = lax.rem(here + step, plane)
        return (lax.div(there, members) * z_len + z, lax.rem(there, members))

    def in_group(step):
        return (g, lax.rem(m + step, members))

    part = points // LOADS
    loads = []
    for i in range(LOADS):
        span = pl.ds(i * part, part)
        loads.append(pltpu.make_async_copy(basis_hbm.at[0, span], basis.at[span], load_sem.at[i]))
    small = [
        pltpu.make_async_copy(src, dst, small_sem.at[i])
        for i, (src, dst) in enumerate(
            [
                (density_hbm, tiles),
                (core_hbm, core_row),
                (weight_hbm, weight_row),
                (pos_hbm, pos_row),
                (ext_hbm, ext_row),
            ]
        )
    ]

    g_up = lax.rem(g + 1, groups)
    tiny = [
        pltpu.make_async_copy(src, dst, index_sem.at[i])
        for i, (src, dst) in enumerate(
            [
                (ids_hbm, ids_ref),
                (extra_hbm, extra_ref),
                (count_hbm, count_ref),
                (live_hbm, live_ref),
            ]
        )
    ]

    barrier = pltpu.get_barrier_semaphore()
    for neighbour in (up, down):
        pl.semaphore_signal(barrier, inc=1, device_id=neighbour, device_id_type=MESH)

    def greet_plane(step, carry):
        pl.semaphore_signal(barrier, inc=1, device_id=in_plane(step), device_id_type=MESH)
        return carry

    def greet_z(step, carry):
        pl.semaphore_signal(barrier, inc=1, device_id=along_z(step), device_id_type=MESH)
        return carry

    lax.fori_loop(1, z_len, greet_z, 0)
    lax.fori_loop(1, plane, greet_plane, 0)
    for copy in tiny:
        copy.start()
    small[0].start()
    for copy in loads:
        copy.start()
    for copy in small[1:]:
        copy.start()

    for copy in tiny:
        copy.wait()
    extra_list = [extra_ref[0, slot] for slot in range(NXT)]
    extra_num = count_ref[0, 0]
    own_places = [
        (place_inner if s < inner_slots else place_cross)(
            ids_ref[m * owned + s, g], extra_list, extra_num
        )
        for s in range(owned)
    ]
    next_places = [
        place_next(ids_ref[m * owned + s, g_up], extra_list, extra_num)
        for s in range(inner_slots)
    ]

    pl.semaphore_wait(barrier, (z_len - 1) + (plane - 1) + 2)

    density_copy = pltpu.make_async_remote_copy(
        src_ref=density_hbm.at[pl.ds(0, inner_slots)],
        dst_ref=arrived,
        send_sem=den_sem.at[0],
        recv_sem=den_sem.at[1],
        device_id=down,
        device_id_type=MESH,
    )
    density_copy.start()

    small[0].wait()
    for s in range(owned):
        factor = own_places[s][3].astype(F32)
        tiles[s] = (tiles[s].astype(F32) * factor).astype(BF16)

    places = own_places + next_places
    firsts = [(0, 0)] * inner_slots + [(0, HOME)] * (owned - inner_slots)
    firsts = firsts + [(HOME, HOME)] * inner_slots

    def tile_terms(span, stack, slots):
        total = None
        for i, s in enumerate(slots):
            _, row, col, _ = places[s]
            block = pick(basis, span, firsts[s][0], row)
            left[s, span, :] = block
            product = jnp.dot(block, stack[i], preferred_element_type=F32)
            term = product * pick(basis, span, firsts[s][1], col).astype(F32)
            total = term if total is None else total + term
        return total

    for i in range(LOADS):
        loads[i].wait()
        span = slice(i * part, (i + 1) * part)
        acc[span, :] = tile_terms(span, tiles, range(owned))
    for copy in small[1:]:
        copy.wait()

    density_copy.wait()
    for s in range(inner_slots):
        factor = next_places[s][3].astype(F32)
        arrived[s] = (arrived[s].astype(F32) * factor).astype(BF16)

    for c in range(points // CHUNK):
        span = slice(c * CHUNK, (c + 1) * CHUNK)
        total = acc[span, :] + tile_terms(span, arrived, range(owned, len(places)))
        for i in range(CHUNK // NB):
            turned = total[i * NB : (i + 1) * NB].T
            at = c * (CHUNK // NB) + i
            rho_own[at : at + 1, :] = jnp.sum(turned, axis=0, keepdims=True)

    rho_part = rho_own[...]
    pos = pos_row[...]
    index = lax.broadcasted_iota(jnp.int32, (rows, NB), 0) * NB + lax.broadcasted_iota(
        jnp.int32, (rows, NB), 1
    )
    live = jnp.where(index < live_ref[0, 0], F32(1.0), F32(0.0))
    live_weight = weight_row[...] * live
    core_share = jnp.where(m == 0, F32(1.0), F32(0.0))
    term = live_weight * (rho_part + core_row[...] * core_share) * F32(1.0 / (groups * points))
    sums = []
    for power in range(NMOM):
        sums.append(jnp.sum(term, axis=0, keepdims=True))
        term = term * pos
    stack = jnp.concatenate(sums + [jnp.zeros((8 - NMOM, NB), F32)], axis=0)
    width = NB // NMOM
    stack = stack + pltpu.roll(stack, NB // 2, 1)
    stack = stack + pltpu.roll(stack, NB // 4, 1)
    quarter = lax.div(lax.broadcasted_iota(jnp.int32, (8, NB), 1), width)
    keep = quarter == lax.broadcasted_iota(jnp.int32, (8, NB), 0)
    row = jnp.sum(jnp.where(keep, stack, F32(0.0)), axis=0, keepdims=True)
    mom_row[...] = row
    mom_slots[z] = row

    def mom_copy(step):
        return pltpu.make_async_remote_copy(
            src_ref=mom_row,
            dst_ref=mom_slots.at[z],
            send_sem=mom_sem.at[0],
            recv_sem=mom_sem.at[1],
            device_id=along_z(step),
            device_id_type=MESH,
        )

    def send_mom(i, carry):
        step = z_len // 2 + lax.div(i + 1, 2) * (1 - 2 * lax.rem(i, 2))
        mom_copy(step).start()
        return carry

    lax.fori_loop(0, z_len - 1, send_mom, 0)

    rho_slots[m] = rho_part

    def rho_copy(step):
        return pltpu.make_async_remote_copy(
            src_ref=rho_own,
            dst_ref=rho_slots.at[m],
            send_sem=rho_sem.at[0],
            recv_sem=rho_sem.at[1],
            device_id=in_group(step),
            device_id_type=MESH,
        )

    def send_rho(step, carry):
        rho_copy(step).start()
        return carry

    lax.fori_loop(1, members, send_rho, 0)

    def wait_all(slots, count, sem, target):
        both = pltpu.make_async_remote_copy(
            src_ref=slots.at[pl.ds(0, count)],
            dst_ref=slots.at[pl.ds(0, count)],
            send_sem=sem.at[0],
            recv_sem=sem.at[1],
            device_id=target,
            device_id_type=MESH,
        )
        return both

    mom_all = wait_all(mom_slots, z_len - 1, mom_sem, along_z(1))
    mom_all.wait_recv()
    column = jnp.sum(mom_slots[...], axis=0)
    part_row[...] = column
    part_slots[here] = column

    def part_copy(step):
        return pltpu.make_async_remote_copy(
            src_ref=part_row,
            dst_ref=part_slots.at[here],
            send_sem=part_sem.at[0],
            recv_sem=part_sem.at[1],
            device_id=in_plane(step),
            device_id_type=MESH,
        )

    def send_part(step, carry):
        part_copy(step).start()
        return carry

    lax.fori_loop(1, plane, send_part, 0)

    def flip_chunk(c, carry):
        span = pl.ds(pl.multiple_of(c * NB, NB), NB)
        for s, (_, _, col, _) in enumerate(places):
            flipped[s, :, span] = pick(basis, span, firsts[s][1], col).T
        return carry

    lax.fori_loop(0, rows, flip_chunk, 0)

    rho_all = wait_all(rho_slots, members - 1, rho_sem, in_group(1))
    rho_all.wait_recv()
    rho = core_row[...] + jnp.sum(rho_slots[...], axis=0)
    local = ext_row[...] - F32(EXCHANGE_COEF) * rho * jnp.exp(
        F32(-1.0 / 3.0) * jnp.log(F32(1.0) + rho * rho)
    )
    scaled_weight = live_weight * F32(1.0 / points)

    part_all = wait_all(part_slots, plane - 1, part_sem, in_plane(1))
    part_all.wait_recv()
    total = jnp.sum(part_slots[...], axis=0)
    lane = lax.div(lax.broadcasted_iota(jnp.int32, (1, NB), 1), width)
    moments = [
        jnp.sum(jnp.where(lane == power, total, F32(0.0)), axis=1, keepdims=True)
        for power in range(NMOM)
    ]
    far = moments[3]
    for power in (2, 1, 0):
        far = far * pos + moments[power]
    potential = local + F32(HARTREE_SCALE) * far
    pot_ref[...] = potential
    pot_out = pltpu.make_async_copy(pot_ref, pot_hbm, out_sem.at[owned])
    pot_out.start()
    quad[...] = scaled_weight * potential

    def ham_tile(s):
        for i in range(rows):
            span = slice(i * NB, (i + 1) * NB)
            block = flipped[s, :, span].astype(F32)
            weighted[:, span] = (block * quad[i : i + 1, :]).astype(BF16)
        turned = jnp.dot(weighted[...], left[s], preferred_element_type=F32)
        return turned.T * places[s][0].astype(F32)

    lent_copies = []
    for s in range(inner_slots):
        lent[s] = ham_tile(owned + s)
        copy = pltpu.make_async_remote_copy(
            src_ref=lent.at[s],
            dst_ref=returned.at[s],
            send_sem=lent_sem.at[0, s],
            recv_sem=lent_sem.at[1, s],
            device_id=up,
            device_id_type=MESH,
        )
        copy.start()
        lent_copies.append(copy)
    ham_out = [
        pltpu.make_async_copy(ham_ref.at[s], ham_hbm.at[s], out_sem.at[s]) for s in range(owned)
    ]
    for s in range(owned):
        ham_ref[s] = ham_tile(s)
        ham_out[s].start()
    for copy in ham_out + [pot_out] + lent_copies:
        copy.wait()

    mom_all.wait_send()
    rho_all.wait_send()
    part_all.wait_send()


def finish(own_hbm, returned_hbm, pot_in, ham_hbm, pot_hbm, own, lent, pot, sem):
    inner_slots = returned_hbm.shape[0]
    first = pl.ds(0, inner_slots)
    others = pl.ds(inner_slots, own_hbm.shape[0] - inner_slots)
    copy = pltpu.make_async_copy
    load_first = copy(own_hbm.at[first], own.at[first], sem.at[0])
    load_lent = copy(returned_hbm, lent, sem.at[1])
    load_others = copy(own_hbm.at[others], own.at[others], sem.at[2])
    load_pot = copy(pot_in, pot, sem.at[3])
    for load in (load_first, load_lent, load_others, load_pot):
        load.start()
    load_first.wait()
    load_lent.wait()
    own[first] = own[first] + lent[...]
    store_first = copy(own.at[first], ham_hbm.at[first], sem.at[4])
    store_first.start()
    load_others.wait()
    store_others = copy(own.at[others], ham_hbm.at[others], sem.at[5])
    store_others.start()
    load_pot.wait()
    store_pot = copy(pot, pot_hbm, sem.at[6])
    store_pot.start()
    for store in (store_first, store_others, store_pot):
        store.wait()


def body(
    basis_values, density, tile_ids, extra_blocks, extra_count, point_count,
    core_density, grid_weights, point_pos, external,
):
    groups = lax.axis_size("batch")
    members = lax.axis_size("blk")
    points = basis_values.shape[1]
    owned = density.shape[0]
    inner_slots = owned // 2
    rows = points // NB
    columns = basis_values.shape[2]
    z_len = min(Z_LEN, groups)
    plane = groups // z_len * members
    hbm = pl.BlockSpec(memory_space=pltpu.HBM)
    own_ham, returned, potential = pl.pallas_call(
        functools.partial(kernel, (groups, members, z_len, points)),
        out_shape=(
            jax.ShapeDtypeStruct((owned, NB, NB), F32),
            jax.ShapeDtypeStruct((inner_slots, NB, NB), F32),
            jax.ShapeDtypeStruct((rows, NB), F32),
        ),
        in_specs=[hbm] * 10,
        out_specs=(hbm, hbm, hbm),
        scratch_shapes=[
            pltpu.SMEM((members * owned, groups), jnp.int32),
            pltpu.SMEM((1, NXT), jnp.int32),
            pltpu.SMEM((1, 1), jnp.int32),
            pltpu.SMEM((1, 1), jnp.int32),
            pltpu.VMEM((points, columns), BF16),
            pltpu.VMEM((owned + inner_slots, points, NB), BF16),
            pltpu.VMEM((owned + inner_slots, NB, points), BF16),
            pltpu.VMEM((owned, NB, NB), BF16),
            pltpu.VMEM((inner_slots, NB, NB), BF16),
            pltpu.VMEM((rows, NB), F32),
            pltpu.VMEM((rows, NB), F32),
            pltpu.VMEM((rows, NB), F32),
            pltpu.VMEM((rows, NB), F32),
            pltpu.VMEM((points, NB), F32),
            pltpu.VMEM((rows, NB), F32),
            pltpu.VMEM((members, rows, NB), F32),
            pltpu.VMEM((1, NB), F32),
            pltpu.VMEM((z_len, 1, NB), F32),
            pltpu.VMEM((1, NB), F32),
            pltpu.VMEM((plane, 1, NB), F32),
            pltpu.VMEM((NB, points), BF16),
            pltpu.VMEM((rows, NB), F32),
            pltpu.VMEM((inner_slots, NB, NB), F32),
            pltpu.VMEM((owned, NB, NB), F32),
            pltpu.VMEM((rows, NB), F32),
            pltpu.SemaphoreType.DMA((LOADS,)),
            pltpu.SemaphoreType.DMA((5,)),
            pltpu.SemaphoreType.DMA((4,)),
            pltpu.SemaphoreType.DMA((2,)),
            pltpu.SemaphoreType.DMA((2,)),
            pltpu.SemaphoreType.DMA((2,)),
            pltpu.SemaphoreType.DMA((2,)),
            pltpu.SemaphoreType.DMA((2, inner_slots)),
            pltpu.SemaphoreType.DMA((owned + 1,)),
        ],
        compiler_params=pltpu.CompilerParams(
            collective_id=0, has_side_effects=True, vmem_limit_bytes=VMEM_BYTES
        ),
        name="density_hamiltonian",
    )(
        tile_ids.T, extra_blocks, extra_count.reshape(1, 1), point_count.reshape(1, 1),
        basis_values, density,
        core_density.reshape(rows, NB), grid_weights.reshape(rows, NB),
        point_pos.reshape(rows, NB), external.reshape(rows, NB),
    )
    ham_tiles, potential = pl.pallas_call(
        finish,
        out_shape=(
            jax.ShapeDtypeStruct((owned, NB, NB), F32),
            jax.ShapeDtypeStruct((rows, NB), F32),
        ),
        in_specs=[hbm] * 3,
        out_specs=(hbm, hbm),
        scratch_shapes=[
            pltpu.VMEM((owned, NB, NB), F32),
            pltpu.VMEM((inner_slots, NB, NB), F32),
            pltpu.VMEM((rows, NB), F32),
            pltpu.SemaphoreType.DMA((7,)),
        ],
        compiler_params=pltpu.CompilerParams(vmem_limit_bytes=VMEM_BYTES),
        name="finish",
    )(own_ham, returned, potential)
    return ham_tiles, potential.reshape(1, points)


def solution(mesh):
    return jax.shard_map(
        body,
        mesh=mesh,
        in_specs=(
            P("batch", None, None),
            P(("batch", "blk"), None, None),
            P(),
            P("batch", None),
            P("batch"),
            P("batch"),
            P("batch", None),
            P("batch", None),
            P("batch", None),
            P("batch", None),
        ),
        out_specs=(P(("batch", "blk"), None, None), P("batch", None)),
        check_vma=False,
    )
```

```python
import functools

import jax
import jax.numpy as jnp
from jax import lax
from jax.experimental import pallas as pl
from jax.experimental.pallas import tpu as pltpu
from jax.sharding import PartitionSpec as P

NB = 128
HOME = 4
NXT = 4
NMOM = 4
Z_LEN = 32
CHUNK = 256
LOADS = 4
VMEM_BYTES = 60 * 1024 * 1024

EXCHANGE_COEF = 0.98
HARTREE_SCALE = 0.5
MESH = pl.DeviceIdType.MESH
F32 = jnp.float32
BF16 = jnp.bfloat16


def next_position(block_id, extra_list, extra_num):
    used = jnp.int32(0)
    position = jnp.int32(0)
    for slot in range(NXT):
        match = jnp.where((extra_list[slot] == block_id) & (slot < extra_num), 1, 0)
        used = used + match
        position = position + match * slot
    return used, position


def place_inner(tile_id, extra_list, extra_num):
    return jnp.int32(1), lax.div(tile_id, HOME), lax.rem(tile_id, HOME), jnp.int32(1)


def place_cross(tile_id, extra_list, extra_num):
    local_id = tile_id - HOME * HOME
    used, position = next_position(lax.rem(local_id, HOME), extra_list, extra_num)
    return used, lax.div(local_id, HOME), position, used * 2


def place_next(tile_id, extra_list, extra_num):
    row_used, row_pos = next_position(lax.div(tile_id, HOME), extra_list, extra_num)
    col_used, col_pos = next_position(lax.rem(tile_id, HOME), extra_list, extra_num)
    is_used = row_used * col_used
    return is_used, row_pos, col_pos, is_used


def pick(ref, span, first, number):
    blocks = [ref[span, (first + b) * NB : (first + b + 1) * NB] for b in range(HOME)]
    out = blocks[0]
    for b in range(1, HOME):
        out = jnp.where(number == b, blocks[b], out)
    return out


def kernel(
    sizes,
    ids_hbm, extra_hbm, count_hbm, live_hbm,
    basis_hbm, density_hbm, core_hbm, weight_hbm, pos_hbm, ext_hbm,
    ham_hbm, returned, pot_hbm,
    ids_ref, extra_ref, count_ref, live_ref,
    basis, left, flipped, tiles, arrived, core_row, weight_row, pos_row, ext_row,
    acc, rho_own, rho_slots, mom_row, mom_slots, part_row, part_slots,
    weighted, quad, lent, ham_ref, pot_ref,
    load_sem, small_sem, index_sem, den_sem, rho_sem, mom_sem, part_sem, lent_sem, out_sem,
):
    groups, members, z_len, points = sizes
    x_len = groups // z_len
    plane = x_len * members
    rows = points // NB
    owned = density_hbm.shape[0]
    inner_slots = owned // 2

    g = lax.axis_index("batch")
    m = lax.axis_index("blk")
    x = lax.div(g, z_len)
    z = lax.rem(g, z_len)
    here = x * members + m
    up = (lax.rem(g + 1, groups), m)
    down = (lax.rem(g + groups - 1, groups), m)

    def far_z(i):
        return z_len // 2 + lax.div(i + 1, 2) * (1 - 2 * lax.rem(i, 2))

    def far_plane(i):
        first = plane // 2 + members - 2
        return lax.rem(first + (plane - 1) - i, plane - 1) + 1

    def along_z(step):
        return (x * z_len + lax.rem(z + step, z_len), m)

    def in_plane(step):
        there = lax.rem(here + step, plane)
        return (lax.div(there, members) * z_len + z, lax.rem(there, members))

    def in_group(step):
        return (g, lax.rem(m + step, members))

    part = points // LOADS
    loads = []
    for i in range(LOADS):
        span = pl.ds(i * part, part)
        loads.append(pltpu.make_async_copy(basis_hbm.at[0, span], basis.at[span], load_sem.at[i]))
    small = [
        pltpu.make_async_copy(src, dst, small_sem.at[i])
        for i, (src, dst) in enumerate(
            [
                (density_hbm, tiles),
                (core_hbm, core_row),
                (weight_hbm, weight_row),
                (pos_hbm, pos_row),
                (ext_hbm, ext_row),
            ]
        )
    ]

    g_up = lax.rem(g + 1, groups)
    tiny = [
        pltpu.make_async_copy(src, dst, index_sem.at[i])
        for i, (src, dst) in enumerate(
            [
                (ids_hbm, ids_ref),
                (extra_hbm, extra_ref),
                (count_hbm, count_ref),
                (live_hbm, live_ref),
            ]
        )
    ]

    barrier = pltpu.get_barrier_semaphore()
    for neighbour in (up, down):
        pl.semaphore_signal(barrier, inc=1, device_id=neighbour, device_id_type=MESH)

    small[0].start()
    for copy in tiny:
        copy.start()
    for copy in loads:
        copy.start()
    for copy in small[1:]:
        copy.start()

    def greet_z(i, carry):
        there = along_z(far_z(i))
        pl.semaphore_signal(barrier, inc=1, device_id=there, device_id_type=MESH)
        return carry

    def greet_plane(i, carry):
        there = in_plane(far_plane(i))
        pl.semaphore_signal(barrier, inc=1, device_id=there, device_id_type=MESH)
        return carry

    lax.fori_loop(0, z_len - 1, greet_z, 0, unroll=True)
    lax.fori_loop(0, plane - 1, greet_plane, 0, unroll=True)
    for copy in tiny:
        copy.wait()
    extra_list = [extra_ref[0, slot] for slot in range(NXT)]
    extra_num = count_ref[0, 0]
    own_places = [
        (place_inner if s < inner_slots else place_cross)(
            ids_ref[m * owned + s, g], extra_list, extra_num
        )
        for s in range(owned)
    ]
    next_places = [
        place_next(ids_ref[m * owned + s, g_up], extra_list, extra_num)
        for s in range(inner_slots)
    ]

    pl.semaphore_wait(barrier, (z_len - 1) + (plane - 1) + 2)

    density_copy = pltpu.make_async_remote_copy(
        src_ref=density_hbm.at[pl.ds(0, inner_slots)],
        dst_ref=arrived,
        send_sem=den_sem.at[0],
        recv_sem=den_sem.at[1],
        device_id=down,
        device_id_type=MESH,
    )
    density_copy.start()

    small[0].wait()
    for s in range(owned):
        factor = own_places[s][3].astype(F32)
        tiles[s] = (tiles[s].astype(F32) * factor).astype(BF16)

    places = own_places + next_places
    firsts = [(0, 0)] * inner_slots + [(0, HOME)] * (owned - inner_slots)
    firsts = firsts + [(HOME, HOME)] * inner_slots

    def tile_terms(span, stack, slots):
        total = None
        for i, s in enumerate(slots):
            _, row, col, _ = places[s]
            block = pick(basis, span, firsts[s][0], row)
            left[s, span, :] = block
            product = jnp.dot(block, stack[i], preferred_element_type=F32)
            term = product * pick(basis, span, firsts[s][1], col).astype(F32)
            total = term if total is None else total + term
        return total

    for i in range(LOADS):
        loads[i].wait()
        span = slice(i * part, (i + 1) * part)
        acc[span, :] = tile_terms(span, tiles, range(owned))
    for copy in small[1:]:
        copy.wait()

    density_copy.wait()
    for s in range(inner_slots):
        factor = next_places[s][3].astype(F32)
        arrived[s] = (arrived[s].astype(F32) * factor).astype(BF16)

    for c in range(points // CHUNK):
        span = slice(c * CHUNK, (c + 1) * CHUNK)
        total = acc[span, :] + tile_terms(span, arrived, range(owned, len(places)))
        for i in range(CHUNK // NB):
            turned = total[i * NB : (i + 1) * NB].T
            at = c * (CHUNK // NB) + i
            rho_own[at : at + 1, :] = jnp.sum(turned, axis=0, keepdims=True)

    rho_part = rho_own[...]
    pos = pos_row[...]
    index = lax.broadcasted_iota(jnp.int32, (rows, NB), 0) * NB + lax.broadcasted_iota(
        jnp.int32, (rows, NB), 1
    )
    live = jnp.where(index < live_ref[0, 0], F32(1.0), F32(0.0))
    live_weight = weight_row[...] * live
    core_share = jnp.where(m == 0, F32(1.0), F32(0.0))
    term = live_weight * (rho_part + core_row[...] * core_share) * F32(1.0 / (groups * points))
    sums = []
    for power in range(NMOM):
        sums.append(jnp.sum(term, axis=0, keepdims=True))
        term = term * pos
    stack = jnp.concatenate(sums + [jnp.zeros((8 - NMOM, NB), F32)], axis=0)
    width = NB // NMOM
    stack = stack + pltpu.roll(stack, NB // 2, 1)
    stack = stack + pltpu.roll(stack, NB // 4, 1)
    quarter = lax.div(lax.broadcasted_iota(jnp.int32, (8, NB), 1), width)
    keep = quarter == lax.broadcasted_iota(jnp.int32, (8, NB), 0)
    row = jnp.sum(jnp.where(keep, stack, F32(0.0)), axis=0, keepdims=True)
    mom_row[...] = row
    mom_slots[z] = row

    def mom_copy(step):
        return pltpu.make_async_remote_copy(
            src_ref=mom_row,
            dst_ref=mom_slots.at[z],
            send_sem=mom_sem.at[0],
            recv_sem=mom_sem.at[1],
            device_id=along_z(step),
            device_id_type=MESH,
        )

    def send_mom(i, carry):
        mom_copy(far_z(i)).start()
        return carry

    lax.fori_loop(0, z_len - 1, send_mom, 0, unroll=True)

    rho_slots[m] = rho_part

    def rho_copy(step):
        return pltpu.make_async_remote_copy(
            src_ref=rho_own,
            dst_ref=rho_slots.at[m],
            send_sem=rho_sem.at[0],
            recv_sem=rho_sem.at[1],
            device_id=in_group(step),
            device_id_type=MESH,
        )

    def send_rho(step, carry):
        rho_copy(step).start()
        return carry

    lax.fori_loop(1, members, send_rho, 0, unroll=True)

    def wait_all(slots, count, sem, target):
        both = pltpu.make_async_remote_copy(
            src_ref=slots.at[pl.ds(0, count)],
            dst_ref=slots.at[pl.ds(0, count)],
            send_sem=sem.at[0],
            recv_sem=sem.at[1],
            device_id=target,
            device_id_type=MESH,
        )
        return both

    mom_all = wait_all(mom_slots, z_len - 1, mom_sem, along_z(1))
    mom_all.wait_recv()
    column = jnp.sum(mom_slots[...], axis=0)
    part_row[...] = column
    part_slots[here] = column

    def part_copy(step):
        return pltpu.make_async_remote_copy(
            src_ref=part_row,
            dst_ref=part_slots.at[here],
            send_sem=part_sem.at[0],
            recv_sem=part_sem.at[1],
            device_id=in_plane(step),
            device_id_type=MESH,
        )

    def send_part(i, carry):
        part_copy(far_plane(i)).start()
        return carry

    lax.fori_loop(0, plane - 1, send_part, 0, unroll=True)

    def flip_chunk(c, carry):
        span = pl.ds(pl.multiple_of(c * NB, NB), NB)
        for s, (_, _, col, _) in enumerate(places):
            flipped[s, :, span] = pick(basis, span, firsts[s][1], col).T
        return carry

    lax.fori_loop(0, rows, flip_chunk, 0)

    rho_all = wait_all(rho_slots, members - 1, rho_sem, in_group(1))
    rho_all.wait_recv()
    rho = core_row[...] + jnp.sum(rho_slots[...], axis=0)
    local = ext_row[...] - F32(EXCHANGE_COEF) * rho * jnp.exp(
        F32(-1.0 / 3.0) * jnp.log(F32(1.0) + rho * rho)
    )
    scaled_weight = live_weight * F32(1.0 / points)

    part_all = wait_all(part_slots, plane - 1, part_sem, in_plane(1))
    part_all.wait_recv()
    total = jnp.sum(part_slots[...], axis=0)
    lane = lax.div(lax.broadcasted_iota(jnp.int32, (1, NB), 1), width)
    moments = [
        jnp.sum(jnp.where(lane == power, total, F32(0.0)), axis=1, keepdims=True)
        for power in range(NMOM)
    ]
    far = moments[3]
    for power in (2, 1, 0):
        far = far * pos + moments[power]
    potential = local + F32(HARTREE_SCALE) * far
    pot_ref[...] = potential
    pot_out = pltpu.make_async_copy(pot_ref, pot_hbm, out_sem.at[owned])
    pot_out.start()
    quad[...] = scaled_weight * potential

    def ham_tile(s):
        for i in range(rows):
            span = slice(i * NB, (i + 1) * NB)
            block = flipped[s, :, span].astype(F32)
            weighted[:, span] = (block * quad[i : i + 1, :]).astype(BF16)
        turned = jnp.dot(weighted[...], left[s], preferred_element_type=F32)
        return turned.T * places[s][0].astype(F32)

    lent_copies = []
    for s in range(inner_slots):
        lent[s] = ham_tile(owned + s)
        copy = pltpu.make_async_remote_copy(
            src_ref=lent.at[s],
            dst_ref=returned.at[s],
            send_sem=lent_sem.at[0, s],
            recv_sem=lent_sem.at[1, s],
            device_id=up,
            device_id_type=MESH,
        )
        lent_copies.append(copy)
        pl.when(g < groups - 1)(copy.start)
    ham_out = [
        pltpu.make_async_copy(ham_ref.at[s], ham_hbm.at[s], out_sem.at[s]) for s in range(owned)
    ]
    for s in range(owned):
        ham_ref[s] = ham_tile(s)
        ham_out[s].start()
    for copy in ham_out + [pot_out]:
        copy.wait()
    for copy in lent_copies:
        pl.when(g < groups - 1)(copy.wait_send)
        pl.when(g > 0)(copy.wait_recv)

    mom_all.wait_send()
    rho_all.wait_send()
    part_all.wait_send()


def finish(own_hbm, returned_hbm, pot_in, ham_hbm, pot_hbm, own, lent, pot, sem):
    inner_slots = returned_hbm.shape[0]
    first = pl.ds(0, inner_slots)
    others = pl.ds(inner_slots, own_hbm.shape[0] - inner_slots)
    copy = pltpu.make_async_copy
    load_first = copy(own_hbm.at[first], own.at[first], sem.at[0])
    load_lent = copy(returned_hbm, lent, sem.at[1])
    load_others = copy(own_hbm.at[others], own.at[others], sem.at[2])
    load_pot = copy(pot_in, pot, sem.at[3])
    for load in (load_first, load_lent, load_others, load_pot):
        load.start()
    load_first.wait()
    load_lent.wait()
    below = lax.axis_index("batch") > 0
    own[first] = own[first] + jnp.where(below, lent[...], F32(0.0))
    store_first = copy(own.at[first], ham_hbm.at[first], sem.at[4])
    store_first.start()
    load_others.wait()
    store_others = copy(own.at[others], ham_hbm.at[others], sem.at[5])
    store_others.start()
    load_pot.wait()
    store_pot = copy(pot, pot_hbm, sem.at[6])
    store_pot.start()
    for store in (store_first, store_others, store_pot):
        store.wait()


def body(
    basis_values, density, tile_ids, extra_blocks, extra_count, point_count,
    core_density, grid_weights, point_pos, external,
):
    groups = lax.axis_size("batch")
    members = lax.axis_size("blk")
    points = basis_values.shape[1]
    owned = density.shape[0]
    inner_slots = owned // 2
    rows = points // NB
    columns = basis_values.shape[2]
    z_len = min(Z_LEN, groups)
    plane = groups // z_len * members
    hbm = pl.BlockSpec(memory_space=pltpu.HBM)
    own_ham, returned, potential = pl.pallas_call(
        functools.partial(kernel, (groups, members, z_len, points)),
        out_shape=(
            jax.ShapeDtypeStruct((owned, NB, NB), F32),
            jax.ShapeDtypeStruct((inner_slots, NB, NB), F32),
            jax.ShapeDtypeStruct((rows, NB), F32),
        ),
        in_specs=[hbm] * 10,
        out_specs=(hbm, hbm, hbm),
        scratch_shapes=[
            pltpu.SMEM((members * owned, groups), jnp.int32),
            pltpu.SMEM((1, NXT), jnp.int32),
            pltpu.SMEM((1, 1), jnp.int32),
            pltpu.SMEM((1, 1), jnp.int32),
            pltpu.VMEM((points, columns), BF16),
            pltpu.VMEM((owned + inner_slots, points, NB), BF16),
            pltpu.VMEM((owned + inner_slots, NB, points), BF16),
            pltpu.VMEM((owned, NB, NB), BF16),
            pltpu.VMEM((inner_slots, NB, NB), BF16),
            pltpu.VMEM((rows, NB), F32),
            pltpu.VMEM((rows, NB), F32),
            pltpu.VMEM((rows, NB), F32),
            pltpu.VMEM((rows, NB), F32),
            pltpu.VMEM((points, NB), F32),
            pltpu.VMEM((rows, NB), F32),
            pltpu.VMEM((members, rows, NB), F32),
            pltpu.VMEM((1, NB), F32),
            pltpu.VMEM((z_len, 1, NB), F32),
            pltpu.VMEM((1, NB), F32),
            pltpu.VMEM((plane, 1, NB), F32),
            pltpu.VMEM((NB, points), BF16),
            pltpu.VMEM((rows, NB), F32),
            pltpu.VMEM((inner_slots, NB, NB), F32),
            pltpu.VMEM((owned, NB, NB), F32),
            pltpu.VMEM((rows, NB), F32),
            pltpu.SemaphoreType.DMA((LOADS,)),
            pltpu.SemaphoreType.DMA((5,)),
            pltpu.SemaphoreType.DMA((4,)),
            pltpu.SemaphoreType.DMA((2,)),
            pltpu.SemaphoreType.DMA((2,)),
            pltpu.SemaphoreType.DMA((2,)),
            pltpu.SemaphoreType.DMA((2,)),
            pltpu.SemaphoreType.DMA((2, inner_slots)),
            pltpu.SemaphoreType.DMA((owned + 1,)),
        ],
        compiler_params=pltpu.CompilerParams(
            collective_id=0, has_side_effects=True, vmem_limit_bytes=VMEM_BYTES
        ),
        name="density_hamiltonian",
    )(
        tile_ids.T, extra_blocks, extra_count.reshape(1, 1), point_count.reshape(1, 1),
        basis_values, density,
        core_density.reshape(rows, NB), grid_weights.reshape(rows, NB),
        point_pos.reshape(rows, NB), external.reshape(rows, NB),
    )
    ham_tiles, potential = pl.pallas_call(
        finish,
        out_shape=(
            jax.ShapeDtypeStruct((owned, NB, NB), F32),
            jax.ShapeDtypeStruct((rows, NB), F32),
        ),
        in_specs=[hbm] * 3,
        out_specs=(hbm, hbm),
        scratch_shapes=[
            pltpu.VMEM((owned, NB, NB), F32),
            pltpu.VMEM((inner_slots, NB, NB), F32),
            pltpu.VMEM((rows, NB), F32),
            pltpu.SemaphoreType.DMA((7,)),
        ],
        compiler_params=pltpu.CompilerParams(vmem_limit_bytes=VMEM_BYTES),
        name="finish",
    )(own_ham, returned, potential)
    return ham_tiles, potential.reshape(1, points)


def solution(mesh):
    return jax.shard_map(
        body,
        mesh=mesh,
        in_specs=(
            P("batch", None, None),
            P(("batch", "blk"), None, None),
            P(),
            P("batch", None),
            P("batch"),
            P("batch"),
            P("batch", None),
            P("batch", None),
            P("batch", None),
            P("batch", None),
        ),
        out_specs=(P(("batch", "blk"), None, None), P("batch", None)),
        check_vma=False,
    )
```

```python
import functools

import jax
import jax.numpy as jnp
from jax import lax
from jax.experimental import pallas as pl
from jax.experimental.pallas import tpu as pltpu
from jax.sharding import PartitionSpec as P

NB = 128
HOME = 4
NXT = 4
NMOM = 4
Z_LEN = 32
CHUNK = 256
LOADS = 4
VMEM_BYTES = 60 * 1024 * 1024

EXCHANGE_COEF = 0.98
HARTREE_SCALE = 0.5
MESH = pl.DeviceIdType.MESH
F32 = jnp.float32
BF16 = jnp.bfloat16


def next_position(block_id, extra_list, extra_num):
    used = jnp.int32(0)
    position = jnp.int32(0)
    for slot in range(NXT):
        match = jnp.where((extra_list[slot] == block_id) & (slot < extra_num), 1, 0)
        used = used + match
        position = position + match * slot
    return used, position


def place_inner(tile_id, extra_list, extra_num):
    return jnp.int32(1), lax.div(tile_id, HOME), lax.rem(tile_id, HOME), jnp.int32(1)


def place_cross(tile_id, extra_list, extra_num):
    local_id = tile_id - HOME * HOME
    used, position = next_position(lax.rem(local_id, HOME), extra_list, extra_num)
    return used, lax.div(local_id, HOME), position, used * 2


def place_next(tile_id, extra_list, extra_num):
    row_used, row_pos = next_position(lax.div(tile_id, HOME), extra_list, extra_num)
    col_used, col_pos = next_position(lax.rem(tile_id, HOME), extra_list, extra_num)
    is_used = row_used * col_used
    return is_used, row_pos, col_pos, is_used


def pick(ref, span, first, number):
    blocks = [ref[span, (first + b) * NB : (first + b + 1) * NB] for b in range(HOME)]
    out = blocks[0]
    for b in range(1, HOME):
        out = jnp.where(number == b, blocks[b], out)
    return out


def kernel(
    sizes,
    ids_hbm, extra_hbm, count_hbm, live_hbm,
    basis_hbm, density_hbm, core_hbm, weight_hbm, pos_hbm, ext_hbm,
    ham_hbm, returned, pot_hbm,
    ids_ref, extra_ref, count_ref, live_ref,
    basis, left, flipped, tiles, arrived, core_row, weight_row, pos_row, ext_row,
    acc, rho_own, rho_slots, mom_row, mom_slots, part_row, part_slots,
    weighted, quad, lent, ham_ref, pot_ref,
    load_sem, small_sem, index_sem, den_sem, rho_sem, mom_sem, part_sem, lent_sem, out_sem,
):
    groups, members, z_len, points = sizes
    x_len = groups // z_len
    plane = x_len * members
    rows = points // NB
    owned = density_hbm.shape[0]
    inner_slots = owned // 2

    g = lax.axis_index("batch")
    m = lax.axis_index("blk")
    x = lax.div(g, z_len)
    z = lax.rem(g, z_len)
    here = x * members + m
    up = (lax.rem(g + 1, groups), m)
    down = (lax.rem(g + groups - 1, groups), m)

    def far_z(i):
        return z_len // 2 + lax.div(i + 1, 2) * (1 - 2 * lax.rem(i, 2))

    def far_plane(i):
        first = plane // 2 + members - 2
        return lax.rem(first + (plane - 1) - i, plane - 1) + 1

    def along_z(step):
        return (x * z_len + lax.rem(z + step, z_len), m)

    def in_plane(step):
        there = lax.rem(here + step, plane)
        return (lax.div(there, members) * z_len + z, lax.rem(there, members))

    def in_group(step):
        return (g, lax.rem(m + step, members))

    part = points // LOADS
    loads = []
    for i in range(LOADS):
        span = pl.ds(i * part, part)
        loads.append(pltpu.make_async_copy(basis_hbm.at[0, span], basis.at[span], load_sem.at[i]))
    small = [
        pltpu.make_async_copy(src, dst, small_sem.at[i])
        for i, (src, dst) in enumerate(
            [
                (density_hbm, tiles),
                (core_hbm, core_row),
                (weight_hbm, weight_row),
                (pos_hbm, pos_row),
                (ext_hbm, ext_row),
            ]
        )
    ]

    g_up = lax.rem(g + 1, groups)
    tiny = [
        pltpu.make_async_copy(src, dst, index_sem.at[i])
        for i, (src, dst) in enumerate(
            [
                (ids_hbm, ids_ref),
                (extra_hbm, extra_ref),
                (count_hbm, count_ref),
                (live_hbm, live_ref),
            ]
        )
    ]

    barrier = pltpu.get_barrier_semaphore()
    for neighbour in (up, down):
        pl.semaphore_signal(barrier, inc=1, device_id=neighbour, device_id_type=MESH)

    small[0].start()
    for copy in tiny:
        copy.start()
    for copy in loads:
        copy.start()
    for copy in small[1:]:
        copy.start()

    def greet_z(i, carry):
        there = along_z(far_z(i))
        pl.semaphore_signal(barrier, inc=1, device_id=there, device_id_type=MESH)
        return carry

    def greet_plane(i, carry):
        there = in_plane(far_plane(i))
        pl.semaphore_signal(barrier, inc=1, device_id=there, device_id_type=MESH)
        return carry

    lax.fori_loop(0, z_len - 1, greet_z, 0, unroll=True)
    lax.fori_loop(0, plane - 1, greet_plane, 0, unroll=True)
    for copy in tiny:
        copy.wait()
    extra_list = [extra_ref[0, slot] for slot in range(NXT)]
    extra_num = count_ref[0, 0]
    own_places = [
        (place_inner if s < inner_slots else place_cross)(
            ids_ref[m * owned + s, g], extra_list, extra_num
        )
        for s in range(owned)
    ]
    next_places = [
        place_next(ids_ref[m * owned + s, g_up], extra_list, extra_num)
        for s in range(inner_slots)
    ]

    pl.semaphore_wait(barrier, (z_len - 1) + (plane - 1) + 2)

    density_copies = [
        pltpu.make_async_remote_copy(
            src_ref=density_hbm.at[s],
            dst_ref=arrived.at[s],
            send_sem=den_sem.at[0, s],
            recv_sem=den_sem.at[1, s],
            device_id=down,
            device_id_type=MESH,
        )
        for s in range(inner_slots)
    ]
    for copy in density_copies:
        copy.start()

    small[0].wait()
    for s in range(owned):
        factor = own_places[s][3].astype(F32)
        tiles[s] = (tiles[s].astype(F32) * factor).astype(BF16)

    places = own_places + next_places
    firsts = [(0, 0)] * inner_slots + [(0, HOME)] * (owned - inner_slots)
    firsts = firsts + [(HOME, HOME)] * inner_slots

    def tile_terms(span, stack, slots):
        total = None
        for i, s in enumerate(slots):
            _, row, col, _ = places[s]
            block = pick(basis, span, firsts[s][0], row)
            left[s, span, :] = block
            product = jnp.dot(block, stack[i], preferred_element_type=F32)
            term = product * pick(basis, span, firsts[s][1], col).astype(F32)
            total = term if total is None else total + term
        return total

    for i in range(LOADS):
        loads[i].wait()
        span = slice(i * part, (i + 1) * part)
        acc[span, :] = tile_terms(span, tiles, range(owned))
    for copy in small[1:]:
        copy.wait()

    for s in range(inner_slots):
        density_copies[s].wait()
        factor = next_places[s][3].astype(F32)
        arrived[s] = (arrived[s].astype(F32) * factor).astype(BF16)
        for c in range(points // CHUNK):
            span = slice(c * CHUNK, (c + 1) * CHUNK)
            total = acc[span, :] + tile_terms(span, arrived.at[pl.ds(s, 1)], [owned + s])
            if s < inner_slots - 1:
                acc[span, :] = total
                continue
            for i in range(CHUNK // NB):
                turned = total[i * NB : (i + 1) * NB].T
                at = c * (CHUNK // NB) + i
                rho_own[at : at + 1, :] = jnp.sum(turned, axis=0, keepdims=True)

    rho_part = rho_own[...]
    pos = pos_row[...]
    index = lax.broadcasted_iota(jnp.int32, (rows, NB), 0) * NB + lax.broadcasted_iota(
        jnp.int32, (rows, NB), 1
    )
    live = jnp.where(index < live_ref[0, 0], F32(1.0), F32(0.0))
    live_weight = weight_row[...] * live
    core_share = jnp.where(m == 0, F32(1.0), F32(0.0))
    term = live_weight * (rho_part + core_row[...] * core_share) * F32(1.0 / (groups * points))
    sums = []
    for power in range(NMOM):
        sums.append(jnp.sum(term, axis=0, keepdims=True))
        term = term * pos
    stack = jnp.concatenate(sums + [jnp.zeros((8 - NMOM, NB), F32)], axis=0)
    width = NB // NMOM
    stack = stack + pltpu.roll(stack, NB // 2, 1)
    stack = stack + pltpu.roll(stack, NB // 4, 1)
    quarter = lax.div(lax.broadcasted_iota(jnp.int32, (8, NB), 1), width)
    keep = quarter == lax.broadcasted_iota(jnp.int32, (8, NB), 0)
    row = jnp.sum(jnp.where(keep, stack, F32(0.0)), axis=0, keepdims=True)
    mom_row[...] = row
    mom_slots[z] = row

    def mom_copy(step):
        return pltpu.make_async_remote_copy(
            src_ref=mom_row,
            dst_ref=mom_slots.at[z],
            send_sem=mom_sem.at[0],
            recv_sem=mom_sem.at[1],
            device_id=along_z(step),
            device_id_type=MESH,
        )

    def send_mom(i, carry):
        mom_copy(far_z(i)).start()
        return carry

    lax.fori_loop(0, z_len - 1, send_mom, 0, unroll=True)

    rho_slots[m] = rho_part

    def rho_copy(step):
        return pltpu.make_async_remote_copy(
            src_ref=rho_own,
            dst_ref=rho_slots.at[m],
            send_sem=rho_sem.at[0],
            recv_sem=rho_sem.at[1],
            device_id=in_group(step),
            device_id_type=MESH,
        )

    def send_rho(step, carry):
        rho_copy(step).start()
        return carry

    lax.fori_loop(1, members, send_rho, 0, unroll=True)

    def wait_all(slots, count, sem, target):
        both = pltpu.make_async_remote_copy(
            src_ref=slots.at[pl.ds(0, count)],
            dst_ref=slots.at[pl.ds(0, count)],
            send_sem=sem.at[0],
            recv_sem=sem.at[1],
            device_id=target,
            device_id_type=MESH,
        )
        return both

    mom_all = wait_all(mom_slots, z_len - 1, mom_sem, along_z(1))
    mom_all.wait_recv()
    column = jnp.sum(mom_slots[...], axis=0)
    part_row[...] = column
    part_slots[here] = column

    def part_copy(step):
        return pltpu.make_async_remote_copy(
            src_ref=part_row,
            dst_ref=part_slots.at[here],
            send_sem=part_sem.at[0],
            recv_sem=part_sem.at[1],
            device_id=in_plane(step),
            device_id_type=MESH,
        )

    def send_part(i, carry):
        part_copy(far_plane(i)).start()
        return carry

    lax.fori_loop(0, plane - 1, send_part, 0, unroll=True)

    def flip_chunk(c, carry):
        span = pl.ds(pl.multiple_of(c * NB, NB), NB)
        for s, (_, _, col, _) in enumerate(places):
            flipped[s, :, span] = pick(basis, span, firsts[s][1], col).T
        return carry

    lax.fori_loop(0, rows, flip_chunk, 0)

    rho_all = wait_all(rho_slots, members - 1, rho_sem, in_group(1))
    rho_all.wait_recv()
    rho = core_row[...] + jnp.sum(rho_slots[...], axis=0)
    local = ext_row[...] - F32(EXCHANGE_COEF) * rho * jnp.exp(
        F32(-1.0 / 3.0) * jnp.log(F32(1.0) + rho * rho)
    )
    scaled_weight = live_weight * F32(1.0 / points)

    part_all = wait_all(part_slots, plane - 1, part_sem, in_plane(1))
    part_all.wait_recv()
    total = jnp.sum(part_slots[...], axis=0)
    lane = lax.div(lax.broadcasted_iota(jnp.int32, (1, NB), 1), width)
    moments = [
        jnp.sum(jnp.where(lane == power, total, F32(0.0)), axis=1, keepdims=True)
        for power in range(NMOM)
    ]
    far = moments[3]
    for power in (2, 1, 0):
        far = far * pos + moments[power]
    potential = local + F32(HARTREE_SCALE) * far
    pot_ref[...] = potential
    pot_out = pltpu.make_async_copy(pot_ref, pot_hbm, out_sem.at[owned])
    pot_out.start()
    quad[...] = scaled_weight * potential

    def ham_tile(s):
        for i in range(rows):
            span = slice(i * NB, (i + 1) * NB)
            block = flipped[s, :, span].astype(F32)
            weighted[:, span] = (block * quad[i : i + 1, :]).astype(BF16)
        turned = jnp.dot(weighted[...], left[s], preferred_element_type=F32)
        return turned.T * places[s][0].astype(F32)

    lent_copies = []
    for s in range(inner_slots):
        lent[s] = ham_tile(owned + s)
        copy = pltpu.make_async_remote_copy(
            src_ref=lent.at[s],
            dst_ref=returned.at[s],
            send_sem=lent_sem.at[0, s],
            recv_sem=lent_sem.at[1, s],
            device_id=up,
            device_id_type=MESH,
        )
        lent_copies.append(copy)
        pl.when(g < groups - 1)(copy.start)
    ham_out = [
        pltpu.make_async_copy(ham_ref.at[s], ham_hbm.at[s], out_sem.at[s]) for s in range(owned)
    ]
    for s in range(owned):
        ham_ref[s] = ham_tile(s)
        ham_out[s].start()
    for copy in ham_out + [pot_out]:
        copy.wait()
    for copy in lent_copies:
        pl.when(g < groups - 1)(copy.wait_send)
        pl.when(g > 0)(copy.wait_recv)

    mom_all.wait_send()
    rho_all.wait_send()
    part_all.wait_send()


def finish(own_hbm, returned_hbm, pot_in, ham_hbm, pot_hbm, own, lent, pot, sem):
    inner_slots = returned_hbm.shape[0]
    owned = own_hbm.shape[0]
    copy = pltpu.make_async_copy
    load_own = [copy(own_hbm.at[s], own.at[s], sem.at[0, s]) for s in range(owned)]
    load_lent = [copy(returned_hbm.at[s], lent.at[s], sem.at[1, s]) for s in range(inner_slots)]
    store = [copy(own.at[s], ham_hbm.at[s], sem.at[2, s]) for s in range(owned)]
    load_pot = copy(pot_in, pot, sem.at[1, inner_slots])
    store_pot = copy(pot, pot_hbm, sem.at[1, inner_slots + 1])
    for s in range(inner_slots):
        load_lent[s].start()
        load_own[s].start()
    for load in load_own[inner_slots:] + [load_pot]:
        load.start()
    below = lax.axis_index("batch") > 0
    for s in range(owned):
        load_own[s].wait()
        if s < inner_slots:
            load_lent[s].wait()
            own[s] = own[s] + jnp.where(below, lent[s], F32(0.0))
        store[s].start()
    load_pot.wait()
    store_pot.start()
    for done in store + [store_pot]:
        done.wait()


def body(
    basis_values, density, tile_ids, extra_blocks, extra_count, point_count,
    core_density, grid_weights, point_pos, external,
):
    groups = lax.axis_size("batch")
    members = lax.axis_size("blk")
    points = basis_values.shape[1]
    owned = density.shape[0]
    inner_slots = owned // 2
    rows = points // NB
    columns = basis_values.shape[2]
    z_len = min(Z_LEN, groups)
    plane = groups // z_len * members
    hbm = pl.BlockSpec(memory_space=pltpu.HBM)
    own_ham, returned, potential = pl.pallas_call(
        functools.partial(kernel, (groups, members, z_len, points)),
        out_shape=(
            jax.ShapeDtypeStruct((owned, NB, NB), F32),
            jax.ShapeDtypeStruct((inner_slots, NB, NB), F32),
            jax.ShapeDtypeStruct((rows, NB), F32),
        ),
        in_specs=[hbm] * 10,
        out_specs=(hbm, hbm, hbm),
        scratch_shapes=[
            pltpu.SMEM((members * owned, groups), jnp.int32),
            pltpu.SMEM((1, NXT), jnp.int32),
            pltpu.SMEM((1, 1), jnp.int32),
            pltpu.SMEM((1, 1), jnp.int32),
            pltpu.VMEM((points, columns), BF16),
            pltpu.VMEM((owned + inner_slots, points, NB), BF16),
            pltpu.VMEM((owned + inner_slots, NB, points), BF16),
            pltpu.VMEM((owned, NB, NB), BF16),
            pltpu.VMEM((inner_slots, NB, NB), BF16),
            pltpu.VMEM((rows, NB), F32),
            pltpu.VMEM((rows, NB), F32),
            pltpu.VMEM((rows, NB), F32),
            pltpu.VMEM((rows, NB), F32),
            pltpu.VMEM((points, NB), F32),
            pltpu.VMEM((rows, NB), F32),
            pltpu.VMEM((members, rows, NB), F32),
            pltpu.VMEM((1, NB), F32),
            pltpu.VMEM((z_len, 1, NB), F32),
            pltpu.VMEM((1, NB), F32),
            pltpu.VMEM((plane, 1, NB), F32),
            pltpu.VMEM((NB, points), BF16),
            pltpu.VMEM((rows, NB), F32),
            pltpu.VMEM((inner_slots, NB, NB), F32),
            pltpu.VMEM((owned, NB, NB), F32),
            pltpu.VMEM((rows, NB), F32),
            pltpu.SemaphoreType.DMA((LOADS,)),
            pltpu.SemaphoreType.DMA((5,)),
            pltpu.SemaphoreType.DMA((4,)),
            pltpu.SemaphoreType.DMA((2, inner_slots)),
            pltpu.SemaphoreType.DMA((2,)),
            pltpu.SemaphoreType.DMA((2,)),
            pltpu.SemaphoreType.DMA((2,)),
            pltpu.SemaphoreType.DMA((2, inner_slots)),
            pltpu.SemaphoreType.DMA((owned + 1,)),
        ],
        compiler_params=pltpu.CompilerParams(
            collective_id=0, has_side_effects=True, vmem_limit_bytes=VMEM_BYTES
        ),
        name="density_hamiltonian",
    )(
        tile_ids.T, extra_blocks, extra_count.reshape(1, 1), point_count.reshape(1, 1),
        basis_values, density,
        core_density.reshape(rows, NB), grid_weights.reshape(rows, NB),
        point_pos.reshape(rows, NB), external.reshape(rows, NB),
    )
    ham_tiles, potential = pl.pallas_call(
        finish,
        out_shape=(
            jax.ShapeDtypeStruct((owned, NB, NB), F32),
            jax.ShapeDtypeStruct((rows, NB), F32),
        ),
        in_specs=[hbm] * 3,
        out_specs=(hbm, hbm),
        scratch_shapes=[
            pltpu.VMEM((owned, NB, NB), F32),
            pltpu.VMEM((inner_slots, NB, NB), F32),
            pltpu.VMEM((rows, NB), F32),
            pltpu.SemaphoreType.DMA((3, owned)),
        ],
        compiler_params=pltpu.CompilerParams(vmem_limit_bytes=VMEM_BYTES),
        name="finish",
    )(own_ham, returned, potential)
    return ham_tiles, potential.reshape(1, points)


def solution(mesh):
    return jax.shard_map(
        body,
        mesh=mesh,
        in_specs=(
            P("batch", None, None),
            P(("batch", "blk"), None, None),
            P(),
            P("batch", None),
            P("batch"),
            P("batch"),
            P("batch", None),
            P("batch", None),
            P("batch", None),
            P("batch", None),
        ),
        out_specs=(P(("batch", "blk"), None, None), P("batch", None)),
        check_vma=False,
    )
```

```python
import functools

import jax
import jax.numpy as jnp
from jax import lax
from jax.experimental import pallas as pl
from jax.experimental.pallas import tpu as pltpu
from jax.sharding import PartitionSpec as P

NB = 128
HOME = 4
NXT = 4
NMOM = 4
Z_LEN = 32
CHUNK = 256
LOADS = 4
VMEM_BYTES = 60 * 1024 * 1024

EXCHANGE_COEF = 0.98
HARTREE_SCALE = 0.5
MESH = pl.DeviceIdType.MESH
F32 = jnp.float32
BF16 = jnp.bfloat16


def next_position(block_id, extra_list, extra_num):
    used = jnp.int32(0)
    position = jnp.int32(0)
    for slot in range(NXT):
        match = jnp.where((extra_list[slot] == block_id) & (slot < extra_num), 1, 0)
        used = used + match
        position = position + match * slot
    return used, position


def place_inner(tile_id, extra_list, extra_num):
    return jnp.int32(1), lax.div(tile_id, HOME), lax.rem(tile_id, HOME), jnp.int32(1)


def place_cross(tile_id, extra_list, extra_num):
    local_id = tile_id - HOME * HOME
    used, position = next_position(lax.rem(local_id, HOME), extra_list, extra_num)
    return used, lax.div(local_id, HOME), position, used * 2


def place_next(tile_id, extra_list, extra_num):
    row_used, row_pos = next_position(lax.div(tile_id, HOME), extra_list, extra_num)
    col_used, col_pos = next_position(lax.rem(tile_id, HOME), extra_list, extra_num)
    is_used = row_used * col_used
    return is_used, row_pos, col_pos, is_used


def pick(ref, span, first, number):
    blocks = [ref[span, (first + b) * NB : (first + b + 1) * NB] for b in range(HOME)]
    out = blocks[0]
    for b in range(1, HOME):
        out = jnp.where(number == b, blocks[b], out)
    return out


def kernel(
    sizes,
    ids_hbm, extra_hbm, count_hbm, live_hbm,
    basis_hbm, density_hbm, core_hbm, weight_hbm, pos_hbm, ext_hbm,
    ham_hbm, returned, pot_hbm,
    ids_ref, extra_ref, count_ref, live_ref,
    basis, left, flipped, tiles, arrived, core_row, weight_row, pos_row, ext_row,
    acc, rho_own, rho_slots, mom_row, mom_slots, part_row, part_slots,
    weighted, quad, lent, ham_ref, pot_ref,
    load_sem, small_sem, index_sem, den_sem, rho_sem, mom_sem, part_sem, lent_sem, out_sem,
):
    groups, members, z_len, points = sizes
    x_len = groups // z_len
    plane = x_len * members
    rows = points // NB
    owned = density_hbm.shape[0]
    inner_slots = owned // 2

    g = lax.axis_index("batch")
    m = lax.axis_index("blk")
    x = lax.div(g, z_len)
    z = lax.rem(g, z_len)
    here = x * members + m
    up = (lax.rem(g + 1, groups), m)
    down = (lax.rem(g + groups - 1, groups), m)

    def far_z(i):
        return z_len // 2 + lax.div(i + 1, 2) * (1 - 2 * lax.rem(i, 2))

    def in_turn(i):
        half = lax.div(i, 2)
        return far_z(half + lax.rem(i, 2) * (z_len - 2 - 2 * half))

    def far_plane(i):
        first = plane // 2 + members - 2
        return lax.rem(first + (plane - 1) - i, plane - 1) + 1

    def along_z(step):
        return (x * z_len + lax.rem(z + step, z_len), m)

    def in_plane(step):
        there = lax.rem(here + step, plane)
        return (lax.div(there, members) * z_len + z, lax.rem(there, members))

    def in_group(step):
        return (g, lax.rem(m + step, members))

    part = points // LOADS
    loads = []
    for i in range(LOADS):
        span = pl.ds(i * part, part)
        loads.append(pltpu.make_async_copy(basis_hbm.at[0, span], basis.at[span], load_sem.at[i]))
    small = [
        pltpu.make_async_copy(src, dst, small_sem.at[i])
        for i, (src, dst) in enumerate(
            [
                (density_hbm, tiles),
                (core_hbm, core_row),
                (weight_hbm, weight_row),
                (pos_hbm, pos_row),
                (ext_hbm, ext_row),
            ]
        )
    ]

    g_up = lax.rem(g + 1, groups)
    tiny = [
        pltpu.make_async_copy(src, dst, index_sem.at[i])
        for i, (src, dst) in enumerate(
            [
                (ids_hbm, ids_ref),
                (extra_hbm, extra_ref),
                (count_hbm, count_ref),
                (live_hbm, live_ref),
            ]
        )
    ]

    barrier = pltpu.get_barrier_semaphore()
    for neighbour in (up, down):
        pl.semaphore_signal(barrier, inc=1, device_id=neighbour, device_id_type=MESH)

    small[0].start()
    for copy in tiny:
        copy.start()
    for copy in loads:
        copy.start()
    for copy in small[1:]:
        copy.start()

    def greet_z(i, carry):
        there = along_z(far_z(i))
        pl.semaphore_signal(barrier, inc=1, device_id=there, device_id_type=MESH)
        return carry

    def greet_plane(i, carry):
        there = in_plane(far_plane(i))
        pl.semaphore_signal(barrier, inc=1, device_id=there, device_id_type=MESH)
        return carry

    lax.fori_loop(0, z_len - 1, greet_z, 0, unroll=True)
    lax.fori_loop(0, plane - 1, greet_plane, 0, unroll=True)
    for copy in tiny:
        copy.wait()
    extra_list = [extra_ref[0, slot] for slot in range(NXT)]
    extra_num = count_ref[0, 0]
    own_places = [
        (place_inner if s < inner_slots else place_cross)(
            ids_ref[m * owned + s, g], extra_list, extra_num
        )
        for s in range(owned)
    ]
    next_places = [
        place_next(ids_ref[m * owned + s, g_up], extra_list, extra_num)
        for s in range(inner_slots)
    ]

    pl.semaphore_wait(barrier, (z_len - 1) + (plane - 1) + 2)

    density_copies = [
        pltpu.make_async_remote_copy(
            src_ref=density_hbm.at[s],
            dst_ref=arrived.at[s],
            send_sem=den_sem.at[0, s],
            recv_sem=den_sem.at[1, s],
            device_id=down,
            device_id_type=MESH,
        )
        for s in range(inner_slots)
    ]
    for copy in density_copies:
        copy.start()

    small[0].wait()
    for s in range(owned):
        factor = own_places[s][3].astype(F32)
        tiles[s] = (tiles[s].astype(F32) * factor).astype(BF16)

    places = own_places + next_places
    firsts = [(0, 0)] * inner_slots + [(0, HOME)] * (owned - inner_slots)
    firsts = firsts + [(HOME, HOME)] * inner_slots

    def tile_terms(span, stack, slots):
        total = None
        for i, s in enumerate(slots):
            _, row, col, _ = places[s]
            block = pick(basis, span, firsts[s][0], row)
            left[s, span, :] = block
            product = jnp.dot(block, stack[i], preferred_element_type=F32)
            term = product * pick(basis, span, firsts[s][1], col).astype(F32)
            total = term if total is None else total + term
        return total

    for i in range(LOADS):
        loads[i].wait()
        span = slice(i * part, (i + 1) * part)
        acc[span, :] = tile_terms(span, tiles, range(owned))
    for copy in small[1:]:
        copy.wait()

    for s in range(inner_slots):
        density_copies[s].wait()
        factor = next_places[s][3].astype(F32)
        arrived[s] = (arrived[s].astype(F32) * factor).astype(BF16)
        for c in range(points // CHUNK):
            span = slice(c * CHUNK, (c + 1) * CHUNK)
            total = acc[span, :] + tile_terms(span, arrived.at[pl.ds(s, 1)], [owned + s])
            if s < inner_slots - 1:
                acc[span, :] = total
                continue
            for i in range(CHUNK // NB):
                turned = total[i * NB : (i + 1) * NB].T
                at = c * (CHUNK // NB) + i
                rho_own[at : at + 1, :] = jnp.sum(turned, axis=0, keepdims=True)

    rho_part = rho_own[...]
    pos = pos_row[...]
    index = lax.broadcasted_iota(jnp.int32, (rows, NB), 0) * NB + lax.broadcasted_iota(
        jnp.int32, (rows, NB), 1
    )
    live = jnp.where(index < live_ref[0, 0], F32(1.0), F32(0.0))
    live_weight = weight_row[...] * live
    core_share = jnp.where(m == 0, F32(1.0), F32(0.0))
    term = live_weight * (rho_part + core_row[...] * core_share) * F32(1.0 / (groups * points))
    sums = []
    for power in range(NMOM):
        sums.append(jnp.sum(term, axis=0, keepdims=True))
        term = term * pos
    stack = jnp.concatenate(sums + [jnp.zeros((8 - NMOM, NB), F32)], axis=0)
    width = NB // NMOM
    stack = stack + pltpu.roll(stack, NB // 2, 1)
    stack = stack + pltpu.roll(stack, NB // 4, 1)
    quarter = lax.div(lax.broadcasted_iota(jnp.int32, (8, NB), 1), width)
    keep = quarter == lax.broadcasted_iota(jnp.int32, (8, NB), 0)
    row = jnp.sum(jnp.where(keep, stack, F32(0.0)), axis=0, keepdims=True)
    mom_row[...] = row
    mom_slots[z] = row

    def mom_copy(step):
        return pltpu.make_async_remote_copy(
            src_ref=mom_row,
            dst_ref=mom_slots.at[z],
            send_sem=mom_sem.at[0],
            recv_sem=mom_sem.at[1],
            device_id=along_z(step),
            device_id_type=MESH,
        )

    def send_mom(i, carry):
        mom_copy(in_turn(i)).start()
        return carry

    lax.fori_loop(0, z_len - 1, send_mom, 0, unroll=True)

    rho_slots[m] = rho_part

    def rho_copy(step):
        return pltpu.make_async_remote_copy(
            src_ref=rho_own,
            dst_ref=rho_slots.at[m],
            send_sem=rho_sem.at[0],
            recv_sem=rho_sem.at[1],
            device_id=in_group(step),
            device_id_type=MESH,
        )

    def send_rho(step, carry):
        rho_copy(step).start()
        return carry

    lax.fori_loop(1, members, send_rho, 0, unroll=True)

    def wait_all(slots, count, sem, target):
        both = pltpu.make_async_remote_copy(
            src_ref=slots.at[pl.ds(0, count)],
            dst_ref=slots.at[pl.ds(0, count)],
            send_sem=sem.at[0],
            recv_sem=sem.at[1],
            device_id=target,
            device_id_type=MESH,
        )
        return both

    mom_all = wait_all(mom_slots, z_len - 1, mom_sem, along_z(1))
    mom_all.wait_recv()
    column = jnp.sum(mom_slots[...], axis=0)
    part_row[...] = column
    part_slots[here] = column

    def part_copy(step):
        return pltpu.make_async_remote_copy(
            src_ref=part_row,
            dst_ref=part_slots.at[here],
            send_sem=part_sem.at[0],
            recv_sem=part_sem.at[1],
            device_id=in_plane(step),
            device_id_type=MESH,
        )

    def send_part(i, carry):
        part_copy(far_plane(i)).start()
        return carry

    lax.fori_loop(0, plane - 1, send_part, 0, unroll=True)

    def flip_chunk(c, carry):
        span = pl.ds(pl.multiple_of(c * NB, NB), NB)
        for s, (_, _, col, _) in enumerate(places):
            flipped[s, :, span] = pick(basis, span, firsts[s][1], col).T
        return carry

    lax.fori_loop(0, rows, flip_chunk, 0)

    rho_all = wait_all(rho_slots, members - 1, rho_sem, in_group(1))
    rho_all.wait_recv()
    rho = core_row[...] + jnp.sum(rho_slots[...], axis=0)
    local = ext_row[...] - F32(EXCHANGE_COEF) * rho * jnp.exp(
        F32(-1.0 / 3.0) * jnp.log(F32(1.0) + rho * rho)
    )
    scaled_weight = live_weight * F32(1.0 / points)

    part_all = wait_all(part_slots, plane - 1, part_sem, in_plane(1))
    part_all.wait_recv()
    total = jnp.sum(part_slots[...], axis=0)
    lane = lax.div(lax.broadcasted_iota(jnp.int32, (1, NB), 1), width)
    moments = [
        jnp.sum(jnp.where(lane == power, total, F32(0.0)), axis=1, keepdims=True)
        for power in range(NMOM)
    ]
    far = moments[3]
    for power in (2, 1, 0):
        far = far * pos + moments[power]
    potential = local + F32(HARTREE_SCALE) * far
    quad[...] = scaled_weight * potential

    def ham_tile(s):
        for i in range(rows):
            span = slice(i * NB, (i + 1) * NB)
            block = flipped[s, :, span].astype(F32)
            weighted[:, span] = (block * quad[i : i + 1, :]).astype(BF16)
        turned = jnp.dot(weighted[...], left[s], preferred_element_type=F32)
        return turned.T * places[s][0].astype(F32)

    lent_copies = []
    for s in range(inner_slots):
        lent[s] = ham_tile(owned + s)
        copy = pltpu.make_async_remote_copy(
            src_ref=lent.at[s],
            dst_ref=returned.at[s],
            send_sem=lent_sem.at[0, s],
            recv_sem=lent_sem.at[1, s],
            device_id=up,
            device_id_type=MESH,
        )
        lent_copies.append(copy)
        pl.when(g < groups - 1)(copy.start)
    pot_ref[...] = potential
    pot_out = pltpu.make_async_copy(pot_ref, pot_hbm, out_sem.at[owned])
    pot_out.start()
    ham_out = [
        pltpu.make_async_copy(ham_ref.at[s], ham_hbm.at[s], out_sem.at[s]) for s in range(owned)
    ]
    for s in range(owned):
        ham_ref[s] = ham_tile(s)
        ham_out[s].start()
    for copy in ham_out + [pot_out]:
        copy.wait()
    for copy in lent_copies:
        pl.when(g < groups - 1)(copy.wait_send)
        pl.when(g > 0)(copy.wait_recv)

    mom_all.wait_send()
    rho_all.wait_send()
    part_all.wait_send()


def finish(own_hbm, returned_hbm, pot_in, ham_hbm, pot_hbm, own, lent, pot, sem):
    inner_slots = returned_hbm.shape[0]
    owned = own_hbm.shape[0]
    copy = pltpu.make_async_copy
    load_own = [copy(own_hbm.at[s], own.at[s], sem.at[0, s]) for s in range(owned)]
    load_lent = [copy(returned_hbm.at[s], lent.at[s], sem.at[1, s]) for s in range(inner_slots)]
    store = [copy(own.at[s], ham_hbm.at[s], sem.at[2, s]) for s in range(owned)]
    load_pot = copy(pot_in, pot, sem.at[1, inner_slots])
    store_pot = copy(pot, pot_hbm, sem.at[1, inner_slots + 1])
    for s in range(inner_slots):
        load_lent[s].start()
        load_own[s].start()
    for load in load_own[inner_slots:] + [load_pot]:
        load.start()
    below = lax.axis_index("batch") > 0
    for s in range(owned):
        load_own[s].wait()
        if s < inner_slots:
            load_lent[s].wait()
            own[s] = own[s] + jnp.where(below, lent[s], F32(0.0))
        store[s].start()
    load_pot.wait()
    store_pot.start()
    for done in store + [store_pot]:
        done.wait()


def body(
    basis_values, density, tile_ids, extra_blocks, extra_count, point_count,
    core_density, grid_weights, point_pos, external,
):
    groups = lax.axis_size("batch")
    members = lax.axis_size("blk")
    points = basis_values.shape[1]
    owned = density.shape[0]
    inner_slots = owned // 2
    rows = points // NB
    columns = basis_values.shape[2]
    z_len = min(Z_LEN, groups)
    plane = groups // z_len * members
    hbm = pl.BlockSpec(memory_space=pltpu.HBM)
    own_ham, returned, potential = pl.pallas_call(
        functools.partial(kernel, (groups, members, z_len, points)),
        out_shape=(
            jax.ShapeDtypeStruct((owned, NB, NB), F32),
            jax.ShapeDtypeStruct((inner_slots, NB, NB), F32),
            jax.ShapeDtypeStruct((rows, NB), F32),
        ),
        in_specs=[hbm] * 10,
        out_specs=(hbm, hbm, hbm),
        scratch_shapes=[
            pltpu.SMEM((members * owned, groups), jnp.int32),
            pltpu.SMEM((1, NXT), jnp.int32),
            pltpu.SMEM((1, 1), jnp.int32),
            pltpu.SMEM((1, 1), jnp.int32),
            pltpu.VMEM((points, columns), BF16),
            pltpu.VMEM((owned + inner_slots, points, NB), BF16),
            pltpu.VMEM((owned + inner_slots, NB, points), BF16),
            pltpu.VMEM((owned, NB, NB), BF16),
            pltpu.VMEM((inner_slots, NB, NB), BF16),
            pltpu.VMEM((rows, NB), F32),
            pltpu.VMEM((rows, NB), F32),
            pltpu.VMEM((rows, NB), F32),
            pltpu.VMEM((rows, NB), F32),
            pltpu.VMEM((points, NB), F32),
            pltpu.VMEM((rows, NB), F32),
            pltpu.VMEM((members, rows, NB), F32),
            pltpu.VMEM((1, NB), F32),
            pltpu.VMEM((z_len, 1, NB), F32),
            pltpu.VMEM((1, NB), F32),
            pltpu.VMEM((plane, 1, NB), F32),
            pltpu.VMEM((NB, points), BF16),
            pltpu.VMEM((rows, NB), F32),
            pltpu.VMEM((inner_slots, NB, NB), F32),
            pltpu.VMEM((owned, NB, NB), F32),
            pltpu.VMEM((rows, NB), F32),
            pltpu.SemaphoreType.DMA((LOADS,)),
            pltpu.SemaphoreType.DMA((5,)),
            pltpu.SemaphoreType.DMA((4,)),
            pltpu.SemaphoreType.DMA((2, inner_slots)),
            pltpu.SemaphoreType.DMA((2,)),
            pltpu.SemaphoreType.DMA((2,)),
            pltpu.SemaphoreType.DMA((2,)),
            pltpu.SemaphoreType.DMA((2, inner_slots)),
            pltpu.SemaphoreType.DMA((owned + 1,)),
        ],
        compiler_params=pltpu.CompilerParams(
            collective_id=0, has_side_effects=True, vmem_limit_bytes=VMEM_BYTES
        ),
        name="density_hamiltonian",
    )(
        tile_ids.T, extra_blocks, extra_count.reshape(1, 1), point_count.reshape(1, 1),
        basis_values, density,
        core_density.reshape(rows, NB), grid_weights.reshape(rows, NB),
        point_pos.reshape(rows, NB), external.reshape(rows, NB),
    )
    ham_tiles, potential = pl.pallas_call(
        finish,
        out_shape=(
            jax.ShapeDtypeStruct((owned, NB, NB), F32),
            jax.ShapeDtypeStruct((rows, NB), F32),
        ),
        in_specs=[hbm] * 3,
        out_specs=(hbm, hbm),
        scratch_shapes=[
            pltpu.VMEM((owned, NB, NB), F32),
            pltpu.VMEM((inner_slots, NB, NB), F32),
            pltpu.VMEM((rows, NB), F32),
            pltpu.SemaphoreType.DMA((3, owned)),
        ],
        compiler_params=pltpu.CompilerParams(vmem_limit_bytes=VMEM_BYTES),
        name="finish",
    )(own_ham, returned, potential)
    return ham_tiles, potential.reshape(1, points)


def solution(mesh):
    return jax.shard_map(
        body,
        mesh=mesh,
        in_specs=(
            P("batch", None, None),
            P(("batch", "blk"), None, None),
            P(),
            P("batch", None),
            P("batch"),
            P("batch"),
            P("batch", None),
            P("batch", None),
            P("batch", None),
            P("batch", None),
        ),
        out_specs=(P(("batch", "blk"), None, None), P("batch", None)),
        check_vma=False,
    )
```

```python
import functools

import jax
import jax.numpy as jnp
from jax import lax
from jax.experimental import pallas as pl
from jax.experimental.pallas import tpu as pltpu
from jax.sharding import PartitionSpec as P

NB = 128
HOME = 4
NXT = 4
NMOM = 4
Z_LEN = 32
CHUNK = 256
LOADS = 4
VMEM_BYTES = 60 * 1024 * 1024

EXCHANGE_COEF = 0.98
HARTREE_SCALE = 0.5
MESH = pl.DeviceIdType.MESH
F32 = jnp.float32
BF16 = jnp.bfloat16


def next_position(block_id, extra_list, extra_num):
    used = jnp.int32(0)
    position = jnp.int32(0)
    for slot in range(NXT):
        match = jnp.where((extra_list[slot] == block_id) & (slot < extra_num), 1, 0)
        used = used + match
        position = position + match * slot
    return used, position


def place_inner(tile_id, extra_list, extra_num):
    return jnp.int32(1), lax.div(tile_id, HOME), lax.rem(tile_id, HOME), jnp.int32(1)


def place_cross(tile_id, extra_list, extra_num):
    local_id = tile_id - HOME * HOME
    used, position = next_position(lax.rem(local_id, HOME), extra_list, extra_num)
    return used, lax.div(local_id, HOME), position, used * 2


def place_next(tile_id, extra_list, extra_num):
    row_used, row_pos = next_position(lax.div(tile_id, HOME), extra_list, extra_num)
    col_used, col_pos = next_position(lax.rem(tile_id, HOME), extra_list, extra_num)
    is_used = row_used * col_used
    return is_used, row_pos, col_pos, is_used


def pick(ref, span, first, number):
    blocks = [ref[span, (first + b) * NB : (first + b + 1) * NB] for b in range(HOME)]
    out = blocks[0]
    for b in range(1, HOME):
        out = jnp.where(number == b, blocks[b], out)
    return out


def kernel(
    sizes,
    ids_hbm, extra_hbm, count_hbm, live_hbm,
    basis_hbm, density_hbm, core_hbm, weight_hbm, pos_hbm, ext_hbm,
    ham_hbm, returned, pot_hbm,
    ids_ref, extra_ref, count_ref, live_ref,
    basis, left, flipped, tiles, arrived, core_row, weight_row, pos_row, ext_row,
    acc, rho_own, rho_slots, mom_row, mom_slots, part_row, part_slots,
    weighted, quad, lent, ham_ref, pot_ref,
    load_sem, small_sem, index_sem, den_sem, rho_sem, mom_sem, part_sem, lent_sem, out_sem,
):
    groups, members, z_len, points = sizes
    x_len = groups // z_len
    plane = x_len * members
    rows = points // NB
    owned = density_hbm.shape[0]
    inner_slots = owned // 2

    g = lax.axis_index("batch")
    m = lax.axis_index("blk")
    x = lax.div(g, z_len)
    z = lax.rem(g, z_len)
    here = x * members + m
    up = (lax.rem(g + 1, groups), m)
    down = (lax.rem(g + groups - 1, groups), m)

    def far_z(i):
        return z_len // 2 + lax.div(i + 1, 2) * (1 - 2 * lax.rem(i, 2))

    def in_turn(i):
        half = lax.div(i, 2)
        return far_z(half + lax.rem(i, 2) * (z_len - 2 - 2 * half))

    def far_plane(i):
        first = plane // 2 + members - 2
        return lax.rem(first + (plane - 1) - i, plane - 1) + 1

    def along_z(step):
        return (x * z_len + lax.rem(z + step, z_len), m)

    def in_plane(step):
        there = lax.rem(here + step, plane)
        return (lax.div(there, members) * z_len + z, lax.rem(there, members))

    def in_group(step):
        return (g, lax.rem(m + step, members))

    part = points // LOADS
    loads = []
    for i in range(LOADS):
        span = pl.ds(i * part, part)
        loads.append(pltpu.make_async_copy(basis_hbm.at[0, span], basis.at[span], load_sem.at[i]))
    small = [
        pltpu.make_async_copy(src, dst, small_sem.at[i])
        for i, (src, dst) in enumerate(
            [
                (density_hbm, tiles),
                (core_hbm, core_row),
                (weight_hbm, weight_row),
                (pos_hbm, pos_row),
                (ext_hbm, ext_row),
            ]
        )
    ]

    g_up = lax.rem(g + 1, groups)
    tiny = [
        pltpu.make_async_copy(src, dst, index_sem.at[i])
        for i, (src, dst) in enumerate(
            [
                (ids_hbm, ids_ref),
                (extra_hbm, extra_ref),
                (count_hbm, count_ref),
                (live_hbm, live_ref),
            ]
        )
    ]

    barrier = pltpu.get_barrier_semaphore()
    for neighbour in (up, down):
        pl.semaphore_signal(barrier, inc=1, device_id=neighbour, device_id_type=MESH)

    small[0].start()
    for copy in tiny:
        copy.start()
    for copy in loads:
        copy.start()
    for copy in small[1:]:
        copy.start()

    def greet_z(i, carry):
        there = along_z(far_z(i))
        pl.semaphore_signal(barrier, inc=1, device_id=there, device_id_type=MESH)
        return carry

    def greet_plane(i, carry):
        there = in_plane(far_plane(i))
        pl.semaphore_signal(barrier, inc=1, device_id=there, device_id_type=MESH)
        return carry

    lax.fori_loop(0, z_len - 1, greet_z, 0, unroll=True)
    lax.fori_loop(0, plane - 1, greet_plane, 0, unroll=True)
    pl.semaphore_wait(barrier, (z_len - 1) + (plane - 1) + 2)

    density_copies = [
        pltpu.make_async_remote_copy(
            src_ref=density_hbm.at[s],
            dst_ref=arrived.at[s],
            send_sem=den_sem.at[0, s],
            recv_sem=den_sem.at[1, s],
            device_id=down,
            device_id_type=MESH,
        )
        for s in range(inner_slots)
    ]
    for copy in density_copies:
        copy.start()

    for copy in tiny:
        copy.wait()
    extra_list = [extra_ref[0, slot] for slot in range(NXT)]
    extra_num = count_ref[0, 0]
    own_places = [
        (place_inner if s < inner_slots else place_cross)(
            ids_ref[m * owned + s, g], extra_list, extra_num
        )
        for s in range(owned)
    ]
    next_places = [
        place_next(ids_ref[m * owned + s, g_up], extra_list, extra_num)
        for s in range(inner_slots)
    ]

    small[0].wait()
    for s in range(owned):
        factor = own_places[s][3].astype(F32)
        tiles[s] = (tiles[s].astype(F32) * factor).astype(BF16)

    places = own_places + next_places
    firsts = [(0, 0)] * inner_slots + [(0, HOME)] * (owned - inner_slots)
    firsts = firsts + [(HOME, HOME)] * inner_slots

    def tile_terms(span, stack, slots):
        total = None
        for i, s in enumerate(slots):
            _, row, col, _ = places[s]
            block = pick(basis, span, firsts[s][0], row)
            left[s, span, :] = block
            product = jnp.dot(block, stack[i], preferred_element_type=F32)
            term = product * pick(basis, span, firsts[s][1], col).astype(F32)
            total = term if total is None else total + term
        return total

    for i in range(LOADS):
        loads[i].wait()
        span = slice(i * part, (i + 1) * part)
        acc[span, :] = tile_terms(span, tiles, range(owned))
    for copy in small[1:]:
        copy.wait()

    for s in range(inner_slots):
        density_copies[s].wait()
        factor = next_places[s][3].astype(F32)
        arrived[s] = (arrived[s].astype(F32) * factor).astype(BF16)
        for c in range(points // CHUNK):
            span = slice(c * CHUNK, (c + 1) * CHUNK)
            total = acc[span, :] + tile_terms(span, arrived.at[pl.ds(s, 1)], [owned + s])
            if s < inner_slots - 1:
                acc[span, :] = total
                continue
            for i in range(CHUNK // NB):
                turned = total[i * NB : (i + 1) * NB].T
                at = c * (CHUNK // NB) + i
                rho_own[at : at + 1, :] = jnp.sum(turned, axis=0, keepdims=True)

    rho_part = rho_own[...]
    pos = pos_row[...]
    index = lax.broadcasted_iota(jnp.int32, (rows, NB), 0) * NB + lax.broadcasted_iota(
        jnp.int32, (rows, NB), 1
    )
    live = jnp.where(index < live_ref[0, 0], F32(1.0), F32(0.0))
    live_weight = weight_row[...] * live
    core_share = jnp.where(m == 0, F32(1.0), F32(0.0))
    term = live_weight * (rho_part + core_row[...] * core_share) * F32(1.0 / (groups * points))
    sums = []
    for power in range(NMOM):
        sums.append(jnp.sum(term, axis=0, keepdims=True))
        term = term * pos
    stack = jnp.concatenate(sums + [jnp.zeros((8 - NMOM, NB), F32)], axis=0)
    width = NB // NMOM
    stack = stack + pltpu.roll(stack, NB // 2, 1)
    stack = stack + pltpu.roll(stack, NB // 4, 1)
    quarter = lax.div(lax.broadcasted_iota(jnp.int32, (8, NB), 1), width)
    keep = quarter == lax.broadcasted_iota(jnp.int32, (8, NB), 0)
    row = jnp.sum(jnp.where(keep, stack, F32(0.0)), axis=0, keepdims=True)
    mom_row[...] = row
    mom_slots[z] = row

    def mom_copy(step):
        return pltpu.make_async_remote_copy(
            src_ref=mom_row,
            dst_ref=mom_slots.at[z],
            send_sem=mom_sem.at[0],
            recv_sem=mom_sem.at[1],
            device_id=along_z(step),
            device_id_type=MESH,
        )

    def send_mom(i, carry):
        mom_copy(in_turn(i)).start()
        return carry

    lax.fori_loop(0, z_len - 1, send_mom, 0, unroll=True)

    rho_slots[m] = rho_part

    def rho_copy(step):
        return pltpu.make_async_remote_copy(
            src_ref=rho_own,
            dst_ref=rho_slots.at[m],
            send_sem=rho_sem.at[0],
            recv_sem=rho_sem.at[1],
            device_id=in_group(step),
            device_id_type=MESH,
        )

    def send_rho(step, carry):
        rho_copy(step).start()
        return carry

    lax.fori_loop(1, members, send_rho, 0, unroll=True)

    def wait_all(slots, count, sem, target):
        both = pltpu.make_async_remote_copy(
            src_ref=slots.at[pl.ds(0, count)],
            dst_ref=slots.at[pl.ds(0, count)],
            send_sem=sem.at[0],
            recv_sem=sem.at[1],
            device_id=target,
            device_id_type=MESH,
        )
        return both

    mom_all = wait_all(mom_slots, z_len - 1, mom_sem, along_z(1))
    mom_all.wait_recv()
    column = jnp.sum(mom_slots[...], axis=0)
    part_row[...] = column
    part_slots[here] = column

    def part_copy(step):
        return pltpu.make_async_remote_copy(
            src_ref=part_row,
            dst_ref=part_slots.at[here],
            send_sem=part_sem.at[0],
            recv_sem=part_sem.at[1],
            device_id=in_plane(step),
            device_id_type=MESH,
        )

    def send_part(i, carry):
        part_copy(far_plane(i)).start()
        return carry

    lax.fori_loop(0, plane - 1, send_part, 0, unroll=True)

    def flip_chunk(c, carry):
        span = pl.ds(pl.multiple_of(c * NB, NB), NB)
        for s, (_, _, col, _) in enumerate(places):
            flipped[s, :, span] = pick(basis, span, firsts[s][1], col).T
        return carry

    lax.fori_loop(0, rows, flip_chunk, 0)

    rho_all = wait_all(rho_slots, members - 1, rho_sem, in_group(1))
    rho_all.wait_recv()
    rho = core_row[...] + jnp.sum(rho_slots[...], axis=0)
    local = ext_row[...] - F32(EXCHANGE_COEF) * rho * jnp.exp(
        F32(-1.0 / 3.0) * jnp.log(F32(1.0) + rho * rho)
    )
    scaled_weight = live_weight * F32(1.0 / points)

    part_all = wait_all(part_slots, plane - 1, part_sem, in_plane(1))
    part_all.wait_recv()
    total = jnp.sum(part_slots[...], axis=0)
    lane = lax.div(lax.broadcasted_iota(jnp.int32, (1, NB), 1), width)
    moments = [
        jnp.sum(jnp.where(lane == power, total, F32(0.0)), axis=1, keepdims=True)
        for power in range(NMOM)
    ]
    far = moments[3]
    for power in (2, 1, 0):
        far = far * pos + moments[power]
    potential = local + F32(HARTREE_SCALE) * far
    quad[...] = scaled_weight * potential

    def ham_tile(s):
        for i in range(rows):
            span = slice(i * NB, (i + 1) * NB)
            block = flipped[s, :, span].astype(F32)
            weighted[:, span] = (block * quad[i : i + 1, :]).astype(BF16)
        turned = jnp.dot(weighted[...], left[s], preferred_element_type=F32)
        return turned.T * places[s][0].astype(F32)

    lent_copies = []
    for s in range(inner_slots):
        lent[s] = ham_tile(owned + s)
        copy = pltpu.make_async_remote_copy(
            src_ref=lent.at[s],
            dst_ref=returned.at[s],
            send_sem=lent_sem.at[0, s],
            recv_sem=lent_sem.at[1, s],
            device_id=up,
            device_id_type=MESH,
        )
        lent_copies.append(copy)
        pl.when(g < groups - 1)(copy.start)
    pot_ref[...] = potential
    pot_out = pltpu.make_async_copy(pot_ref, pot_hbm, out_sem.at[owned])
    pot_out.start()
    ham_out = [
        pltpu.make_async_copy(ham_ref.at[s], ham_hbm.at[s], out_sem.at[s]) for s in range(owned)
    ]
    for s in range(owned):
        ham_ref[s] = ham_tile(s)
        ham_out[s].start()
    for copy in ham_out + [pot_out]:
        copy.wait()
    mom_all.wait_send()
    rho_all.wait_send()
    part_all.wait_send()
    for copy in lent_copies:
        pl.when(g < groups - 1)(copy.wait_send)
        pl.when(g > 0)(copy.wait_recv)


def finish(own_hbm, returned_hbm, pot_in, ham_hbm, pot_hbm, own, lent, pot, sem):
    inner_slots = returned_hbm.shape[0]
    owned = own_hbm.shape[0]
    copy = pltpu.make_async_copy
    load_own = [copy(own_hbm.at[s], own.at[s], sem.at[0, s]) for s in range(owned)]
    load_lent = [copy(returned_hbm.at[s], lent.at[s], sem.at[1, s]) for s in range(inner_slots)]
    store = [copy(own.at[s], ham_hbm.at[s], sem.at[2, s]) for s in range(owned)]
    load_pot = copy(pot_in, pot, sem.at[1, inner_slots])
    store_pot = copy(pot, pot_hbm, sem.at[1, inner_slots + 1])
    for s in range(inner_slots):
        load_lent[s].start()
        load_own[s].start()
    for load in load_own[inner_slots:] + [load_pot]:
        load.start()
    below = lax.axis_index("batch") > 0
    for s in range(owned):
        load_own[s].wait()
        if s < inner_slots:
            load_lent[s].wait()
            own[s] = own[s] + jnp.where(below, lent[s], F32(0.0))
        store[s].start()
    load_pot.wait()
    store_pot.start()
    for done in store + [store_pot]:
        done.wait()


def body(
    basis_values, density, tile_ids, extra_blocks, extra_count, point_count,
    core_density, grid_weights, point_pos, external,
):
    groups = lax.axis_size("batch")
    members = lax.axis_size("blk")
    points = basis_values.shape[1]
    owned = density.shape[0]
    inner_slots = owned // 2
    rows = points // NB
    columns = basis_values.shape[2]
    z_len = min(Z_LEN, groups)
    plane = groups // z_len * members
    hbm = pl.BlockSpec(memory_space=pltpu.HBM)
    own_ham, returned, potential = pl.pallas_call(
        functools.partial(kernel, (groups, members, z_len, points)),
        out_shape=(
            jax.ShapeDtypeStruct((owned, NB, NB), F32),
            jax.ShapeDtypeStruct((inner_slots, NB, NB), F32),
            jax.ShapeDtypeStruct((rows, NB), F32),
        ),
        in_specs=[hbm] * 10,
        out_specs=(hbm, hbm, hbm),
        scratch_shapes=[
            pltpu.SMEM((members * owned, groups), jnp.int32),
            pltpu.SMEM((1, NXT), jnp.int32),
            pltpu.SMEM((1, 1), jnp.int32),
            pltpu.SMEM((1, 1), jnp.int32),
            pltpu.VMEM((points, columns), BF16),
            pltpu.VMEM((owned + inner_slots, points, NB), BF16),
            pltpu.VMEM((owned + inner_slots, NB, points), BF16),
            pltpu.VMEM((owned, NB, NB), BF16),
            pltpu.VMEM((inner_slots, NB, NB), BF16),
            pltpu.VMEM((rows, NB), F32),
            pltpu.VMEM((rows, NB), F32),
            pltpu.VMEM((rows, NB), F32),
            pltpu.VMEM((rows, NB), F32),
            pltpu.VMEM((points, NB), F32),
            pltpu.VMEM((rows, NB), F32),
            pltpu.VMEM((members, rows, NB), F32),
            pltpu.VMEM((1, NB), F32),
            pltpu.VMEM((z_len, 1, NB), F32),
            pltpu.VMEM((1, NB), F32),
            pltpu.VMEM((plane, 1, NB), F32),
            pltpu.VMEM((NB, points), BF16),
            pltpu.VMEM((rows, NB), F32),
            pltpu.VMEM((inner_slots, NB, NB), F32),
            pltpu.VMEM((owned, NB, NB), F32),
            pltpu.VMEM((rows, NB), F32),
            pltpu.SemaphoreType.DMA((LOADS,)),
            pltpu.SemaphoreType.DMA((5,)),
            pltpu.SemaphoreType.DMA((4,)),
            pltpu.SemaphoreType.DMA((2, inner_slots)),
            pltpu.SemaphoreType.DMA((2,)),
            pltpu.SemaphoreType.DMA((2,)),
            pltpu.SemaphoreType.DMA((2,)),
            pltpu.SemaphoreType.DMA((2, inner_slots)),
            pltpu.SemaphoreType.DMA((owned + 1,)),
        ],
        compiler_params=pltpu.CompilerParams(
            collective_id=0, has_side_effects=True, vmem_limit_bytes=VMEM_BYTES
        ),
        name="density_hamiltonian",
    )(
        tile_ids.T, extra_blocks, extra_count.reshape(1, 1), point_count.reshape(1, 1),
        basis_values, density,
        core_density.reshape(rows, NB), grid_weights.reshape(rows, NB),
        point_pos.reshape(rows, NB), external.reshape(rows, NB),
    )
    ham_tiles, potential = pl.pallas_call(
        finish,
        out_shape=(
            jax.ShapeDtypeStruct((owned, NB, NB), F32),
            jax.ShapeDtypeStruct((rows, NB), F32),
        ),
        in_specs=[hbm] * 3,
        out_specs=(hbm, hbm),
        scratch_shapes=[
            pltpu.VMEM((owned, NB, NB), F32),
            pltpu.VMEM((inner_slots, NB, NB), F32),
            pltpu.VMEM((rows, NB), F32),
            pltpu.SemaphoreType.DMA((3, owned)),
        ],
        compiler_params=pltpu.CompilerParams(vmem_limit_bytes=VMEM_BYTES),
        name="finish",
    )(own_ham, returned, potential)
    return ham_tiles, potential.reshape(1, points)


def solution(mesh):
    return jax.shard_map(
        body,
        mesh=mesh,
        in_specs=(
            P("batch", None, None),
            P(("batch", "blk"), None, None),
            P(),
            P("batch", None),
            P("batch"),
            P("batch"),
            P("batch", None),
            P("batch", None),
            P("batch", None),
            P("batch", None),
        ),
        out_specs=(P(("batch", "blk"), None, None), P("batch", None)),
        check_vma=False,
    )
```
